128 devices in a mesh: gz: 32 (over y_hi, x, z), gy: 4 (over y_lo, core).
Axes of the slice: x: 4, y: 4 (y_hi: 2, y_lo: 2; y = y_hi * 2 + y_lo), z: 4, core: 2. Of those that a mesh axis runs over, the one named last changes fastest.
Arguments:
- state: float32 [9, 512, 64, 256], P(None, 'gz', 'gy'), may hold values from -6 to 6
- region: int32 [512, 64, 256], P('gz', 'gy'), may hold values from 0 to 7
- lame_table: float32 [8], replicated, may hold values from 0.5 to 2
- shear_table: float32 [8], replicated, may hold values from 0.3 to 1
- buoyancy_table: float32 [8], replicated, may hold values from 0.5 to 1.5
- face_block: int32 [32, 4, 32], P('gz', 'gy'), may hold values from 0 to 511, as said below
- face_owner: int32 [32, 4, 32], P('gz', 'gy'), may hold values from 0 to 31, as said below
- face_slot: int32 [32, 4, 32], P('gz', 'gy'), may hold values from 0 to 31, as said below
- joint_gain: float32 [32, 4, 16], P('gz', 'gy'), may hold values from 0.2 to 0.9
Outputs:
- final_state: float32 [9, 512, 64, 256], P(None, 'gz', 'gy')
- sensitivity: float32 [3, 512, 64, 256], P(None, 'gz', 'gy')
The draws below stay inside these ranges and needn't reach their ends.
Inputs may be any that keep to these rules, and one draw needn't show every extreme that they name: `face_block`: within one device the blocks are distinct. `face_owner`: each device sends either none or exactly 2 faces to each owner; every owner receives 32 faces. `face_slot`: among the faces sent to one owner (same gy index) every slot 0 to 31 occurs exactly once.
All inputs are finite; a program needn't handle non-finite values.
Results may differ from the reference program's by a relative error of at most 0.000054.
Values sent between devices are 32-bit elements; how exact they have to be, the bound alone decides.
A program may use at most 64 MiB of HBM per device.

```python
import math
import jax
import jax.numpy as jnp
from jax import lax

NX = 256
CY = 16
CZ = 16
STEPS = 12
CAP = 2
REGIONS = 8
NZ = 512
NY = 64
FACES = 32
JOINT_DEV = 16
N_GZ = 32
N_GY = 4


def joint_lists(key):
    groups = NZ // CZ
    columns = NY // CY
    blocks_dev = CZ * CY * (NX // 128)
    block_keys = jax.random.split(jax.random.fold_in(key, 101), groups * columns)
    blocks = jax.vmap(lambda subkey: jax.random.permutation(subkey, blocks_dev)[:FACES])(block_keys)
    blocks = blocks.reshape(groups, columns, FACES).astype(jnp.int32)
    shift_keys = jax.random.split(jax.random.fold_in(key, 102), columns)
    shifts = jax.vmap(lambda subkey: jax.random.permutation(subkey, groups)[:FACES // CAP])(shift_keys).astype(jnp.int32)
    perm_keys = jax.random.split(jax.random.fold_in(key, 103), groups * columns)
    perms = jax.vmap(lambda subkey: jax.random.permutation(subkey, FACES))(perm_keys).reshape(groups, columns, FACES).astype(jnp.int32)
    source = jnp.arange(groups, dtype=jnp.int32)[:, None, None]
    column = jnp.arange(columns, dtype=jnp.int32)[None, :, None]
    face_ids = jnp.arange(FACES, dtype=jnp.int32)[None, None, :]
    owner = (source + shifts[column, face_ids // CAP]) % groups
    slot = perms[owner, jnp.broadcast_to(column, owner.shape), jnp.broadcast_to(face_ids, owner.shape)]
    return (blocks, owner.astype(jnp.int32), slot.astype(jnp.int32))


def draw_face_block(key, part):
    return joint_lists(key)[0]


def draw_face_owner(key, part):
    return joint_lists(key)[1]


def draw_face_slot(key, part):
    return joint_lists(key)[2]


def plant(values, rng, least, high):
    spot = [jax.random.randint(jax.random.fold_in(rng, axis), (), 0, length) for axis, length in enumerate(values.shape)]
    main_axis = values.shape.index(max(values.shape))
    beside = spot[:main_axis] + [(spot[main_axis] + 1) % values.shape[main_axis]] + spot[main_axis + 1:]
    return values.at[tuple(spot)].set(least).at[tuple(beside)].set(high)


def shard_levels(rng, dims, cuts, smallest, high):
    def one(axis_at, shards_of):
        steps = jax.random.uniform(jax.random.fold_in(jax.random.fold_in(rng, 6), axis_at), (shards_of,), jnp.float32, smallest / len(cuts), high / len(cuts))
        return jnp.repeat(jnp.exp(steps), dims[axis_at] // shards_of).reshape((-1,) + (1,) * (len(dims) - axis_at - 1))

    gain = one(*cuts[0])
    for cut in cuts[1:]:
        gain = gain * one(*cut)
    return gain


def centred(rng, dims, deviation, limit, cuts=(), kind=jnp.bfloat16):
    array = jax.random.normal(rng, dims, jnp.float32) * deviation
    if len(cuts) > 0:
        array = shard_levels(rng, dims, cuts, -0.22, 0.18) * array
    return jnp.clip(array, min=-limit, max=limit).astype(kind)


def setup_inputs(seed: int = 0) -> dict:
    streams_of = jax.random.split(jax.random.key(seed), 10)
    state = centred(streams_of[0], (9, NZ, NY, NX), 1.0, 6.0, ((1, 32), (2, 4)), jnp.float32)
    region = plant(jax.random.randint(streams_of[1], (NZ, NY, NX), 0, REGIONS), jax.random.fold_in(streams_of[1], 1), 0, REGIONS - 1).astype(jnp.int32)
    lame_table = jnp.clip(jax.random.uniform(streams_of[2], (REGIONS,), jnp.float32, 0.5, 2.0), 0.5, 2.0)
    shear_table = jnp.clip(jax.random.uniform(streams_of[3], (REGIONS,), jnp.float32, 0.3, 1.0), 0.3, 1.0)
    buoyancy_table = jnp.clip(jax.random.uniform(streams_of[4], (REGIONS,), jnp.float32, 0.5, 1.5), 0.5, 1.5)
    face_block = draw_face_block(jax.random.fold_in(streams_of[9], 71), 0)
    face_owner = draw_face_owner(jax.random.fold_in(streams_of[9], 71), 0)
    face_slot = draw_face_slot(jax.random.fold_in(streams_of[9], 71), 0)
    joint_gain = jnp.clip(jnp.exp(math.log(0.9) - 1.50407736 * jax.random.uniform(streams_of[8], (N_GZ, N_GY, JOINT_DEV), jnp.float32) ** shard_levels(streams_of[8], (N_GZ, N_GY, JOINT_DEV), ((0, 32), (1, 4)), -0.2, 0.2)), 0.2, 0.9)
    return {"state": state, "region": region, "lame_table": lame_table, "shear_table": shear_table, "buoyancy_table": buoyancy_table, "face_block": face_block, "face_owner": face_owner, "face_slot": face_slot, "joint_gain": joint_gain}


c_near = 9.0 / 8.0
c_far = -1.0 / 24.0
time_step = 0.15
lane_width = 128

def difference(padded, axis, forward):
    length = padded.shape[axis] - 4

    def window(offset):
        return lax.slice_in_dim(padded, offset, offset + length, axis=axis)
    if forward:
        return c_near * (window(3) - window(2)) + c_far * (window(4) - window(1))
    return c_near * (window(2) - window(1)) + c_far * (window(3) - window(0))

def padded_along(field, axis):
    widths = [(0, 0), (0, 0), (0, 0)]
    widths[axis] = (2, 2)
    return jnp.pad(field, widths)

def velocity_update(vel, stress, buoy, y_rims, z_rims):
    force_x = difference(padded_along(stress[0], 2), 2, True) + difference(y_rims[1], 1, False) + difference(z_rims[2], 0, False)
    force_y = difference(padded_along(stress[2], 2), 2, False) + difference(y_rims[0], 1, True) + difference(z_rims[0], 0, False)
    force_z = difference(padded_along(stress[5], 2), 2, False) + difference(y_rims[2], 1, False) + difference(z_rims[1], 0, True)
    return jnp.stack([vel[0] + time_step * buoy * force_x, vel[1] + time_step * buoy * force_y, vel[2] + time_step * buoy * force_z])

def stress_update(vel, stress, lame, shear, y_rims, z_rims):
    strain_x = difference(padded_along(vel[0], 2), 2, False)
    strain_y = difference(y_rims[1], 1, False)
    strain_z = difference(z_rims[2], 0, False)
    dilation = strain_x + strain_y + strain_z
    new_xx = stress[0] + time_step * (lame * dilation + 2.0 * shear * strain_x)
    new_yy = stress[1] + time_step * (lame * dilation + 2.0 * shear * strain_y)
    new_zz = stress[4] + time_step * (lame * dilation + 2.0 * shear * strain_z)
    new_xy = stress[2] + time_step * shear * (difference(y_rims[0], 1, True) + difference(padded_along(vel[1], 2), 2, True))
    new_yz = stress[3] + time_step * shear * (difference(z_rims[1], 0, True) + difference(y_rims[2], 1, True))
    new_xz = stress[5] + time_step * shear * (difference(z_rims[0], 0, True) + difference(padded_along(vel[2], 2), 2, True))
    return jnp.stack([new_xx, new_yy, new_xy, new_yz, new_zz, new_xz])

def couple(vel, face_block, face_owner, face_slot, joint_gain):
    groups, columns, faces = face_block.shape
    per_row = NX // lane_width
    source = jnp.arange(groups, dtype=jnp.int32)[:, None, None]
    column = jnp.arange(columns, dtype=jnp.int32)[None, :, None]
    z_pos = source * CZ + face_block // (CY * per_row)
    y_pos = column * CY + face_block // per_row % CY
    x_start = face_block % per_row * lane_width
    lanes = jnp.arange(lane_width, dtype=jnp.int32)
    z_index = z_pos[..., None]
    y_index = y_pos[..., None]
    x_index = x_start[..., None] + lanes
    picked = jnp.moveaxis(vel[:, z_index, y_index, x_index], 0, 3)
    joint = face_slot // 2
    side = face_slot % 2
    column_all = jnp.broadcast_to(column, face_slot.shape)
    table = jnp.zeros((groups, columns, faces // 2, 2, 3, lane_width), jnp.float32)
    table = table.at[face_owner, column_all, joint, side].set(picked)
    slip = table[:, :, :, 0] - table[:, :, :, 1]
    traction = joint_gain[..., None, None] * slip / jnp.sqrt(1.0 + slip * slip)
    halves = jnp.stack([-0.5 * traction, 0.5 * traction], axis=3)
    returned = halves[face_owner, column_all, joint, side]
    return vel.at[:, z_index, y_index, x_index].add(jnp.moveaxis(returned, 3, 0))

def reference(state, region, lame_table, shear_table, buoyancy_table, face_block, face_owner, face_slot, joint_gain):
    lame = lame_table[region]
    shear = shear_table[region]
    buoy = buoyancy_table[region]
    vel = state[0:3]
    stress = state[3:9]
    sens = jnp.zeros_like(vel)
    y_widths = ((0, 0), (0, 0), (2, 2), (0, 0))
    z_widths = ((0, 0), (2, 2), (0, 0), (0, 0))
    for step_index in range(STEPS):
        y_rims = jnp.pad(stress[1:4], y_widths)
        z_rims = jnp.pad(stress[3:6], z_widths)
        vel = velocity_update(vel, stress, buoy, y_rims, z_rims)
        vel = couple(vel, face_block, face_owner, face_slot, joint_gain)
        stress = stress_update(vel, stress, lame, shear, jnp.pad(vel, y_widths), jnp.pad(vel, z_widths))
        sens = sens + time_step * vel
    return (jnp.concatenate([vel, stress], axis=0), sens)
```

```python
import jax
import jax.numpy as jnp
from jax import lax
from jax.sharding import PartitionSpec as P
from jax.experimental import pallas as pl
from jax.experimental.pallas import tpu as pltpu

MESH = pl.DeviceIdType.MESH
STEPS = 12
CAP = 2
C1 = 9.0 / 8.0
C2 = -1.0 / 24.0
DT = 0.15
NGZ, NGY = 32, 4
CZ, CY, XB, LANE = 16, 16, 2, 128
POS = NGZ * CAP
YR, Y0 = 40, 10
VZ, V0 = CZ + 8, 4
SZ, S0 = CZ + 4, 2
F32 = jnp.float32
BF16 = jnp.bfloat16

OFFSETS = sorted(
    [(a, b, c) for a in range(2) for b in range(4) for c in range(4) if a + b + c > 0],
    key=lambda o: -(2 * o[0] + min(o[1], 4 - o[1]) + min(o[2], 4 - o[2])),
)


def xshift(f0, f1, by):
    lane = lax.broadcasted_iota(jnp.int32, f0.shape, 1)
    a = pltpu.roll(f0, (-by) % LANE, 1)
    b = pltpu.roll(f1, (-by) % LANE, 1)
    if by > 0:
        keep = lane < LANE - by
        return jnp.where(keep, a, b), jnp.where(keep, b, 0.0)
    keep = lane >= -by
    return jnp.where(keep, a, 0.0), jnp.where(keep, b, a)


def stencil(p, c, n, f, forward):
    return C1 * (n - c) + C2 * (f - p)


def dx(f0, f1, forward):
    up = xshift(f0, f1, 1)
    dn = xshift(f0, f1, -1)
    if forward:
        far = xshift(f0, f1, 2)
        return tuple(C1 * (up[i] - (f0, f1)[i]) + C2 * (far[i] - dn[i]) for i in range(2))
    far = xshift(f0, f1, -2)
    return tuple(C1 * ((f0, f1)[i] - dn[i]) + C2 * (up[i] - far[i]) for i in range(2))


def dmaj(load, forward):
    if forward:
        return C1 * (load(1) - load(0)) + C2 * (load(2) - load(-1))
    return C1 * (load(0) - load(-1)) + C2 * (load(1) - load(-2))


def kernel(
    state, region, lame, shear, buoyt, meta, bpos, gain,
    out, sens_out,
    V, S, own, dtb, sens, reg, bsend, brecv, csend, crecv, htab, onehot, rhs,
    mrecv, gtab, gs, srcv, srcs,
    lsem, bs, br, cs, cr, zs, zr, ys, yr, ms, mr, hs, hr,
):
    gz = lax.axis_index("gz")
    gy = lax.axis_index("gy")
    a0, b0, c0 = gz // 16, (gz // 4) % 4, gz % 4
    partners = [
        ((a0 + a) % 2) * 16 + ((b0 + b) % 4) * 4 + (c0 + c) % 4 for a, b, c in OFFSETS
    ]
    down, up = (gz + NGZ - 1) % NGZ, (gz + 1) % NGZ
    left, right = (gy + NGY - 1) % NGY, (gy + 1) % NGY
    has = {"down": gz > 0, "up": gz < NGZ - 1, "left": gy > 0, "right": gy < NGY - 1}

    zero = jnp.zeros((8, LANE), F32)

    def clear_v(l, c):
        for par in range(2):
            for f in range(3):
                for xb in range(XB):
                    for t in range(YR // 8):
                        V[par, f, l, xb, pl.ds(8 * t, 8), :] = zero
        return c

    lax.fori_loop(0, VZ, clear_v, 0)

    def clear_s(l, c):
        for f in range(8):
            for xb in range(XB):
                for t in range(YR // 8):
                    S[f, l, xb, pl.ds(8 * t, 8), :] = zero
        return c

    lax.fori_loop(0, SZ, clear_s, 0)

    def clear_c(l, c):
        csend[l] = zero
        return c

    lax.fori_loop(0, POS + 4, clear_c, 0)
    htab[32] = zero
    for f in range(3):
        rhs[f, 192:256, :] = jnp.zeros((64, 384), BF16)

    loads = []
    for xb in range(XB):
        cols = pl.ds(xb * LANE, LANE)
        loads.append(pltpu.make_async_copy(region.at[:, :, cols], reg.at[:, xb], lsem.at[0, xb]))
        loads.append(
            pltpu.make_async_copy(
                state.at[0:3, :, :, cols], V.at[0, :, V0 : V0 + CZ, xb, Y0 : Y0 + CY, :], lsem.at[1, xb]
            )
        )
        loads.append(
            pltpu.make_async_copy(
                state.at[3:9, :, :, cols], S.at[0:6, S0 : S0 + CZ, xb, Y0 : Y0 + CY, :], lsem.at[2, xb]
            )
        )
    for cp in loads:
        cp.start()

    barrier = pltpu.get_barrier_semaphore()
    for t in partners:
        pl.semaphore_signal(barrier, inc=1, device_id=(t, gy), device_id_type=MESH)
    for t in range(1, NGY):
        pl.semaphore_signal(barrier, inc=1, device_id=(gz, (gy + t) % NGY), device_id_type=MESH)

    for cp in loads:
        cp.wait()

    def material(l, c):
        for xb in range(XB):
            r = reg[l, xb]
            la = jnp.zeros((CY, LANE), F32)
            mu = jnp.zeros((CY, LANE), F32)
            bu = jnp.zeros((CY, LANE), F32)
            for v in range(8):
                hit = r == v
                la = jnp.where(hit, DT * lame[v], la)
                mu = jnp.where(hit, DT * shear[v], mu)
                bu = jnp.where(hit, DT * buoyt[v], bu)
            S[6, S0 + l, xb, pl.ds(Y0, CY), :] = la
            S[7, S0 + l, xb, pl.ds(Y0, CY), :] = mu
            dtb[l, xb] = bu
            for f in range(3):
                sens[f, l, xb] = jnp.zeros((CY, LANE), F32)
        return c

    lax.fori_loop(0, CZ, material, 0)
    pl.semaphore_wait(barrier, NGZ - 1 + NGY - 1)

    def remote(src, dst, s, r, to):
        return pltpu.make_async_remote_copy(
            src, dst, send_sem=s, recv_sem=r, device_id=to, device_id_type=MESH
        )

    def meta_copy(t):
        return remote(meta.at[0:2], mrecv.at[gz, 0:2], ms, mr, (t, gy))

    for t in partners:
        meta_copy(t).start()
    mrecv[gz] = meta[...]

    first = {
        "down": remote(S.at[3:8, 2:4, :, 10:26], S.at[3:8, 18:20, :, 10:26], hs.at[0], hr.at[0], (down, gy)),
        "up": remote(S.at[3:8, 16:18, :, 10:26], S.at[3:8, 0:2, :, 10:26], hs.at[1], hr.at[1], (up, gy)),
        "left": remote(S.at[1:4, 2:18, :, 10:12], S.at[1:4, 2:18, :, 26:28], hs.at[2], hr.at[2], (gz, left)),
        "right": remote(S.at[1:4, 2:18, :, 24:26], S.at[1:4, 2:18, :, 8:10], hs.at[3], hr.at[3], (gz, right)),
        "left2": remote(S.at[6:8, 2:18, :, 10:12], S.at[6:8, 2:18, :, 26:28], hs.at[4], hr.at[4], (gz, left)),
        "right2": remote(S.at[6:8, 2:18, :, 24:26], S.at[6:8, 2:18, :, 8:10], hs.at[5], hr.at[5], (gz, right)),
    }
    opposite = {"down": "up", "up": "down", "left": "right", "right": "left"}

    def start(copies):
        for name, cp in copies.items():
            pl.when(has[name.rstrip("2")])(cp.start)

    def wait_send(copies):
        for name, cp in copies.items():
            pl.when(has[name.rstrip("2")])(cp.wait_send)

    def wait_recv(copies):
        for name, cp in copies.items():
            pl.when(has[opposite[name.rstrip("2")]])(cp.wait_recv)

    start(first)

    all31 = mrecv.at[0 : NGZ - 1, 0:2]
    pltpu.make_async_copy(all31, all31, ms).wait()
    pltpu.make_async_copy(all31, all31, mr).wait()

    lane = lax.broadcasted_iota(jnp.int32, (NGZ, LANE), 1)
    dev = lax.broadcasted_iota(jnp.int32, (NGZ, LANE), 0)
    got = mrecv[:, 1, :]
    gtab[...] = got
    mine = (lane >= 2 * gz) & (lane < 2 * gz + 2)
    got = jnp.where(mine, got, -1)
    place = 2 * dev + lane - 2 * gz
    lane1 = lax.broadcasted_iota(jnp.int32, (8, LANE), 1)
    acc = jnp.zeros((8, LANE), jnp.int32)
    for s in range(32):
        total = jnp.sum(jnp.where(got == s, place, 0))
        acc = jnp.where(lane1 == s, total, acc)
    srcv[...] = jnp.minimum(acc, POS - 1)
    c1 = pltpu.make_async_copy(gtab, gs, lsem.at[0, 0])
    c2 = pltpu.make_async_copy(srcv, srcs, lsem.at[0, 1])
    c1.start()
    c2.start()

    row = lax.broadcasted_iota(jnp.int32, (CY, LANE), 0)
    lane16 = lax.broadcasted_iota(jnp.int32, (CY, LANE), 1)

    def ones(l, c):
        z = jnp.where(l < 3, l + 13, jnp.where(l < 19, l - 3, l - 19))
        who = jnp.where(l < 3, gz - 1, jnp.where(l < 19, gz, gz + 1))
        real = (who >= 0) & (who < NGZ)
        blk = mrecv[jnp.clip(who, 0, NGZ - 1), 0:1, :]
        blk = jnp.where(real, blk, -1)
        for xb in range(XB):
            hit = blk == z * 32 + row * 2 + xb
            start_row = pl.multiple_of(l * 32 + xb * 16, 16)
            onehot[pl.ds(start_row, 16), 0:128] = jnp.where(hit, 1.0, 0.0).astype(BF16)
            onehot[pl.ds(start_row, 16), 128:256] = jnp.where(hit & (lane16 < 64), 1.0, 0.0).astype(BF16)
        return c

    lax.fori_loop(0, CZ + 6, ones, 0)
    c1.wait()
    c2.wait()
    wait_send(first)
    wait_recv(first)

    def step(n, carry):
        p = lax.rem(n, 2)
        q = 1 - p

        def velocity(k, c):
            ks = k + S0
            for t in range(2):
                r0 = Y0 + 8 * t

                def s(f, xb, dz=0, dy=0):
                    return S[f, ks + dz, xb, pl.ds(r0 + dy, 8), :]

                xx = dx(s(0, 0), s(0, 1), True)
                xy = dx(s(2, 0), s(2, 1), False)
                xz = dx(s(5, 0), s(5, 1), False)
                for xb in range(XB):
                    fx = xx[xb] + dmaj(lambda o: s(2, xb, dy=o), False) + dmaj(lambda o: s(5, xb, dz=o), False)
                    fy = xy[xb] + dmaj(lambda o: s(1, xb, dy=o), True) + dmaj(lambda o: s(3, xb, dz=o), False)
                    fz = xz[xb] + dmaj(lambda o: s(3, xb, dy=o), False) + dmaj(lambda o: s(4, xb, dz=o), True)
                    bu = dtb[k, xb, pl.ds(8 * t, 8), :]
                    for f, force in enumerate((fx, fy, fz)):
                        new = V[p, f, k + V0, xb, pl.ds(r0, 8), :] + bu * force
                        V[q, f, k + V0, xb, pl.ds(r0, 8), :] = new
                        own[f, k, xb, pl.ds(8 * t, 8), :] = new
            return c

        lax.fori_loop(0, CZ, velocity, 0)

        def pick(i, c):
            for u in range(4):
                e = i * 4 + u
                b = bpos[0, 0, e]
                z, y, xb = b // 32, (b // 2) % 16, b % 2
                for f in range(3):
                    bsend[e, pl.ds(f, 1), :] = own[f, z, xb, pl.ds(y, 1), :]
            return c

        lax.fori_loop(0, POS // 4, pick, 0)

        def b_copy(t):
            return remote(
                bsend.at[pl.ds(2 * t, 2), 0:3], brecv.at[pl.ds(2 * gz, 2), 0:3], bs, br, (t, gy)
            )

        for t in partners:
            b_copy(t).start()
        for u in range(2):
            brecv[2 * gz + u] = bsend[2 * gz + u]

        zc = {
            "down": remote(V.at[q, :, 4:7, :, 10:26], V.at[q, :, 20:23, :, 10:26], zs.at[0], zr.at[q, 0], (down, gy)),
            "up": remote(V.at[q, :, 17:20, :, 10:26], V.at[q, :, 1:4, :, 10:26], zs.at[1], zr.at[q, 1], (up, gy)),
        }
        start(zc)

        ball = brecv.at[0 : POS - 2, 0:3]
        pltpu.make_async_copy(ball, ball, br).wait()

        for j in range(16):
            side0 = brecv[srcs[0, 2 * j]]
            side1 = brecv[srcs[0, 2 * j + 1]]
            slip = side0 - side1
            traction = gain[0, 0, j] * slip / jnp.sqrt(1.0 + slip * slip)
            htab[2 * j] = -0.5 * traction
            htab[2 * j + 1] = 0.5 * traction

        def reply(d, c):
            for u in range(2):
                slot = gs[d, 2 * gz + u]
                slot = jnp.where((slot < 0) | (slot > 32), 32, slot)
                csend[2 * d + 2 + u] = htab[slot]
            return c

        lax.fori_loop(0, NGZ, reply, 0)

        def c_copy(t):
            return remote(csend.at[pl.ds(2 * t, 6), 0:3], crecv.at[gz, :, 0:3], cs, cr, (t, gy))

        for t in partners:
            c_copy(t).start()
        for u in range(6):
            crecv[gz, u] = csend[2 * gz + u]

        pltpu.make_async_copy(ball, ball, bs).wait()
        wait_send(zc)
        wait_recv(zc)
        call = crecv.at[0 : NGZ - 1, :, 0:3]
        pltpu.make_async_copy(call, call, cr).wait()

        for g in range(3):
            for f in range(3):
                col = pl.ds(f * LANE, LANE)
                d = crecv[:, 2 * g : 2 * g + 2, f, :].reshape(POS, LANE)
                hi = d.astype(BF16)
                d = d - hi.astype(F32)
                mid = d.astype(BF16)
                lo = (d - mid.astype(F32)).astype(BF16)
                rhs[g, 0:64, col] = hi
                rhs[g, 64:128, col] = mid
                rhs[g, 128:192, col] = lo

        def apply(first_layer, layers, g):
            start_row = first_layer * 32
            if not isinstance(start_row, int):
                start_row = pl.multiple_of(start_row, 32)
            delta = jnp.dot(
                onehot[pl.ds(start_row, layers * 32), :], rhs[g], preferred_element_type=F32
            )
            for l in range(layers):
                for xb in range(XB):
                    for f in range(3):
                        r = l * 32 + xb * 16
                        here = V[q, f, first_layer + 1 + l, xb, pl.ds(Y0, CY), :]
                        V[q, f, first_layer + 1 + l, xb, pl.ds(Y0, CY), :] = (
                            here + delta[r : r + 16, f * LANE : (f + 1) * LANE]
                        )

        apply(0, 3, 0)
        apply(19, 3, 2)

        def apply_own(i, c):
            apply(3 + 4 * i, 4, 1)
            return c

        lax.fori_loop(0, 4, apply_own, 0)
        pltpu.make_async_copy(call, call, cs).wait()

        yc = {
            "left": remote(V.at[q, :, 1:23, :, 10:13], V.at[q, :, 1:23, :, 26:29], ys.at[0], yr.at[q, 0], (gz, left)),
            "right": remote(V.at[q, :, 1:23, :, 23:26], V.at[q, :, 1:23, :, 7:10], ys.at[1], yr.at[q, 1], (gz, right)),
        }
        start(yc)

        def sensitivity(k, c):
            for f in range(3):
                for xb in range(XB):
                    sens[f, k, xb] = sens[f, k, xb] + DT * V[q, f, k + V0, xb, pl.ds(Y0, CY), :]
            return c

        lax.fori_loop(0, CZ, sensitivity, 0)
        wait_send(yc)
        wait_recv(yc)

        def stress(k, c):
            kv = k + 2
            for t in range(3):
                r0 = 8 + 8 * t

                def v(f, xb, dz=0, dy=0):
                    return V[q, f, kv + dz, xb, pl.ds(r0 + dy, 8), :]

                exs = dx(v(0, 0), v(0, 1), False)
                vyx = dx(v(1, 0), v(1, 1), True)
                vzx = dx(v(2, 0), v(2, 1), True)
                for xb in range(XB):
                    ex = exs[xb]
                    ey = dmaj(lambda o: v(1, xb, dy=o), False)
                    ez = dmaj(lambda o: v(2, xb, dz=o), False)
                    la = S[6, k, xb, pl.ds(r0, 8), :]
                    mu = S[7, k, xb, pl.ds(r0, 8), :]
                    mu2 = mu + mu
                    div = la * (ex + ey + ez)
                    new = (
                        div + mu2 * ex,
                        div + mu2 * ey,
                        mu * (dmaj(lambda o: v(0, xb, dy=o), True) + vyx[xb]),
                        mu * (dmaj(lambda o: v(1, xb, dz=o), True) + dmaj(lambda o: v(2, xb, dy=o), True)),
                        div + mu2 * ez,
                        mu * (dmaj(lambda o: v(0, xb, dz=o), True) + vzx[xb]),
                    )
                    for f in range(6):
                        S[f, k, xb, pl.ds(r0, 8), :] = S[f, k, xb, pl.ds(r0, 8), :] + new[f]
            return c

        lax.fori_loop(0, SZ, stress, 0)
        return carry

    lax.fori_loop(0, STEPS, step, 0)

    last = STEPS % 2
    stores = []
    for xb in range(XB):
        cols = pl.ds(xb * LANE, LANE)
        stores.append(
            pltpu.make_async_copy(
                V.at[last, :, V0 : V0 + CZ, xb, Y0 : Y0 + CY, :], out.at[0:3, :, :, cols], lsem.at[0, xb]
            )
        )
        stores.append(
            pltpu.make_async_copy(
                S.at[0:6, S0 : S0 + CZ, xb, Y0 : Y0 + CY, :], out.at[3:9, :, :, cols], lsem.at[1, xb]
            )
        )
        stores.append(pltpu.make_async_copy(sens.at[:, :, xb], sens_out.at[:, :, :, cols], lsem.at[2, xb]))
    for cp in stores:
        cp.start()
    for cp in stores:
        cp.wait()


def per_device(state, region, lame, shear, buoyt, face_block, face_owner, face_slot, joint_gain):
    blocks, owners, slots = face_block.reshape(-1), face_owner.reshape(-1), face_slot.reshape(-1)
    ids = jnp.arange(blocks.shape[0], dtype=jnp.int32)
    earlier = (owners[None, :] == owners[:, None]) & (ids[None, :] < ids[:, None])
    position = owners * CAP + jnp.sum(earlier.astype(jnp.int32), axis=1)
    match = jnp.arange(POS, dtype=jnp.int32)[:, None] == position[None, :]
    block_at = jnp.sum(jnp.where(match, blocks[None, :] + 1, 0), axis=1) - 1
    slot_at = jnp.sum(jnp.where(match, slots[None, :] + 1, 0), axis=1) - 1
    meta = jnp.concatenate([block_at, block_at, slot_at, slot_at]).reshape(2, LANE)
    meta = jnp.concatenate([meta, jnp.zeros((6, LANE), jnp.int32)], axis=0)
    bpos = jnp.maximum(block_at, 0).reshape(1, 1, POS)
    smem = pl.BlockSpec(memory_space=pltpu.SMEM)
    vmem = pl.BlockSpec(memory_space=pltpu.VMEM)
    anym = pl.BlockSpec(memory_space=pl.ANY)
    dma = pltpu.SemaphoreType.DMA
    return pl.pallas_call(
        kernel,
        out_shape=(
            jax.ShapeDtypeStruct(state.shape, F32),
            jax.ShapeDtypeStruct((3,) + state.shape[1:], F32),
        ),
        in_specs=[anym, anym, smem, smem, smem, vmem, smem, smem],
        out_specs=(anym, anym),
        scratch_shapes=[
            pltpu.VMEM((2, 3, VZ, XB, YR, LANE), F32),
            pltpu.VMEM((8, SZ, XB, YR, LANE), F32),
            pltpu.VMEM((3, CZ, XB, CY, LANE), F32),
            pltpu.VMEM((CZ, XB, CY, LANE), F32),
            pltpu.VMEM((3, CZ, XB, CY, LANE), F32),
            pltpu.VMEM((CZ, XB, CY, LANE), jnp.int32),
            pltpu.VMEM((POS, 8, LANE), F32),
            pltpu.VMEM((POS, 8, LANE), F32),
            pltpu.VMEM((POS + 4, 8, LANE), F32),
            pltpu.VMEM((NGZ, 6, 8, LANE), F32),
            pltpu.VMEM((33, 8, LANE), F32),
            pltpu.VMEM(((CZ + 6) * 32, 256), BF16),
            pltpu.VMEM((3, 256, 3 * LANE), BF16),
            pltpu.VMEM((NGZ, 8, LANE), jnp.int32),
            pltpu.VMEM((NGZ, LANE), jnp.int32),
            pltpu.SMEM((NGZ, LANE), jnp.int32),
            pltpu.VMEM((8, LANE), jnp.int32),
            pltpu.SMEM((8, LANE), jnp.int32),
            dma((3, 2)),
            dma,
            dma,
            dma,
            dma,
            dma((2,)),
            dma((2, 2)),
            dma((2,)),
            dma((2, 2)),
            dma,
            dma,
            dma((6,)),
            dma((6,)),
        ],
        compiler_params=pltpu.CompilerParams(
            collective_id=0, has_side_effects=True, vmem_limit_bytes=40 * 1024 * 1024
        ),
    )(state, region, lame, shear, buoyt, meta, bpos, joint_gain)


def solution(mesh):
    grid = P("gz", "gy", None)
    field = P(None, "gz", "gy", None)
    return jax.shard_map(
        per_device,
        mesh=mesh,
        in_specs=(field, grid, P(), P(), P(), grid, grid, grid, grid),
        out_specs=(field, field),
        check_vma=False,
    )
```

```python
import functools

import jax
import jax.numpy as jnp
from jax import lax
from jax.sharding import PartitionSpec as P
from jax.experimental import pallas as pl
from jax.experimental.pallas import tpu as pltpu

MESH = pl.DeviceIdType.MESH
STEPS = 12
CAP = 2
C1 = 9.0 / 8.0
C2 = -1.0 / 24.0
DT = 0.15
NGZ, NGY = 32, 4
CZ, CY, XB, LANE = 16, 16, 2, 128
POS = NGZ * CAP
YR, Y0 = 40, 14
VZ, V0 = CZ + 8, 4
SZ, S0 = CZ + 4, 2
F32 = jnp.float32
BF16 = jnp.bfloat16

OFFSETS = sorted(
    [(a, b, c) for a in range(2) for b in range(4) for c in range(4) if a + b + c > 0],
    key=lambda o: -(2 * o[0] + min(o[1], 4 - o[1]) + min(o[2], 4 - o[2])),
)


def xshift(f0, f1, by):
    lane = lax.broadcasted_iota(jnp.int32, f0.shape, 1)
    a = pltpu.roll(f0, (-by) % LANE, 1)
    b = pltpu.roll(f1, (-by) % LANE, 1)
    if by > 0:
        keep = lane < LANE - by
        return jnp.where(keep, a, b), jnp.where(keep, b, 0.0)
    keep = lane >= -by
    return jnp.where(keep, a, 0.0), jnp.where(keep, b, a)


def stencil(p, c, n, f, forward):
    return C1 * (n - c) + C2 * (f - p)


def dx(f0, f1, forward):
    up = xshift(f0, f1, 1)
    dn = xshift(f0, f1, -1)
    if forward:
        far = xshift(f0, f1, 2)
        return tuple(C1 * (up[i] - (f0, f1)[i]) + C2 * (far[i] - dn[i]) for i in range(2))
    far = xshift(f0, f1, -2)
    return tuple(C1 * ((f0, f1)[i] - dn[i]) + C2 * (up[i] - far[i]) for i in range(2))


def dmaj(load, forward):
    if forward:
        return C1 * (load(1) - load(0)) + C2 * (load(2) - load(-1))
    return C1 * (load(0) - load(-1)) + C2 * (load(1) - load(-2))


def kernel(
    state, region, lame, shear, buoyt, fblock, fowner, fslot, gain,
    out, sens_out,
    V, S, own, dtb, sens, reg, bsend, brecv, csend, crecv, htab, onehot, rhs,
    meta, mrecv, gtab, gs, srcv, srcs, bposv, bpos,
    lsem, bs, br, cs, cr, zs, zr, ys, yr, ms, mr, hs, hr,
):
    gz = lax.axis_index("gz")
    gy = lax.axis_index("gy")
    a0, b0, c0 = gz // 16, (gz // 4) % 4, gz % 4
    partners = [
        ((a0 + a) % 2) * 16 + ((b0 + b) % 4) * 4 + (c0 + c) % 4 for a, b, c in OFFSETS
    ]
    down, up = (gz + NGZ - 1) % NGZ, (gz + 1) % NGZ
    left, right = (gy + NGY - 1) % NGY, (gy + 1) % NGY
    has = {"down": gz > 0, "up": gz < NGZ - 1, "left": gy > 0, "right": gy < NGY - 1}

    loads = []
    for xb in range(XB):
        cols = pl.ds(xb * LANE, LANE)
        loads.append(pltpu.make_async_copy(region.at[:, :, cols], reg.at[:, xb], lsem.at[0, xb]))
        loads.append(
            pltpu.make_async_copy(
                state.at[0:3, :, :, cols], V.at[0, :, V0 : V0 + CZ, xb, Y0 : Y0 + CY, :], lsem.at[1, xb]
            )
        )
        loads.append(
            pltpu.make_async_copy(
                state.at[3:9, :, :, cols], S.at[0:6, S0 : S0 + CZ, xb, Y0 : Y0 + CY, :], lsem.at[2, xb]
            )
        )
    for cp in loads:
        cp.start()

    zero = jnp.zeros((8, LANE), F32)
    zero16 = jnp.zeros((CY, LANE), F32)

    def edges(ref, idx):
        for xb in range(XB):
            ref[(*idx, xb, pl.ds(Y0 - 8, 8), slice(None))] = zero
            ref[(*idx, xb, pl.ds(Y0 + CY, 8), slice(None))] = zero

    def clear_v(l, c):
        for par in range(2):
            for f in range(3):
                edges(V, (par, f, l))
        return c

    lax.fori_loop(0, VZ, clear_v, 0)

    def clear_s(l, c):
        for f in range(8):
            edges(S, (f, l))
        return c

    lax.fori_loop(0, SZ, clear_s, 0)

    def clear_layers(l, c):
        for xb in range(XB):
            for base in (0, V0 + CZ):
                for par in range(2):
                    for f in range(3):
                        V[par, f, base + l, xb, pl.ds(Y0, CY), :] = zero16
        return c

    lax.fori_loop(0, V0, clear_layers, 0)
    for l in (0, 1, S0 + CZ, S0 + CZ + 1):
        for xb in range(XB):
            for f in range(8):
                S[f, l, xb, pl.ds(Y0, CY), :] = zero16
    for f in range(3):
        csend[f, 0:8, :] = zero
        csend[f, 64:72, :] = zero
        rhs[f, 192:256, :] = jnp.zeros((64, 384), BF16)
    htab[32] = zero

    lane8 = lax.broadcasted_iota(jnp.int32, (8, LANE), 1)
    lane_owner, lane_rank = lane8 % 32, (lane8 // 32) % 2
    count = jnp.zeros((8, LANE), jnp.int32)
    block_at = jnp.full((8, LANE), -1, jnp.int32)
    slot_at = jnp.full((8, LANE), -1, jnp.int32)
    for e in range(32):
        to = lane_owner == fowner[0, 0, e]
        here = to & (lane_rank == count)
        block_at = jnp.where(here, fblock[0, 0, e], block_at)
        slot_at = jnp.where(here, fslot[0, 0, e], slot_at)
        count = jnp.where(to, count + 1, count)
    sub = lax.broadcasted_iota(jnp.int32, (8, LANE), 0)
    meta[...] = jnp.where(sub == 0, block_at, slot_at)
    bposv[...] = jnp.clip(block_at, 0, 511)

    barrier = pltpu.get_barrier_semaphore()
    for t in partners:
        pl.semaphore_signal(barrier, inc=1, device_id=(t, gy), device_id_type=MESH)
    for t in range(1, NGY):
        pl.semaphore_signal(barrier, inc=1, device_id=(gz, (gy + t) % NGY), device_id_type=MESH)

    for cp in loads:
        cp.wait()

    def material(l, c):
        for xb in range(XB):
            r = reg[l, xb]
            la = jnp.zeros((CY, LANE), F32)
            mu = jnp.zeros((CY, LANE), F32)
            bu = jnp.zeros((CY, LANE), F32)
            for v in range(8):
                hit = r == v
                la = jnp.where(hit, DT * lame[v], la)
                mu = jnp.where(hit, DT * shear[v], mu)
                bu = jnp.where(hit, DT * buoyt[v], bu)
            S[6, S0 + l, xb, pl.ds(Y0, CY), :] = la
            S[7, S0 + l, xb, pl.ds(Y0, CY), :] = mu
            dtb[l, xb] = bu
            for f in range(3):
                sens[f, l, xb] = jnp.zeros((CY, LANE), F32)
        return c

    lax.fori_loop(0, CZ, material, 0)
    pl.semaphore_wait(barrier, NGZ - 1 + NGY - 1)

    def remote(src, dst, s, r, to):
        return pltpu.make_async_remote_copy(
            src, dst, send_sem=s, recv_sem=r, device_id=to, device_id_type=MESH
        )

    def meta_copy(t):
        return remote(meta.at[0:2], mrecv.at[gz, 0:2], ms, mr, (t, gy))

    for t in partners:
        meta_copy(t).start()
    mrecv[gz] = meta[...]

    first = {
        "down": remote(S.at[3:8, 2:4, :, 14:30], S.at[3:8, 18:20, :, 14:30], hs.at[0], hr.at[0], (down, gy)),
        "up": remote(S.at[3:8, 16:18, :, 14:30], S.at[3:8, 0:2, :, 14:30], hs.at[1], hr.at[1], (up, gy)),
        "left": remote(S.at[1:4, 2:18, :, 14:16], S.at[1:4, 2:18, :, 30:32], hs.at[2], hr.at[2], (gz, left)),
        "right": remote(S.at[1:4, 2:18, :, 28:30], S.at[1:4, 2:18, :, 12:14], hs.at[3], hr.at[3], (gz, right)),
        "left2": remote(S.at[6:8, 2:18, :, 14:16], S.at[6:8, 2:18, :, 30:32], hs.at[4], hr.at[4], (gz, left)),
        "right2": remote(S.at[6:8, 2:18, :, 28:30], S.at[6:8, 2:18, :, 12:14], hs.at[5], hr.at[5], (gz, right)),
    }
    opposite = {"down": "up", "up": "down", "left": "right", "right": "left"}

    def start(copies):
        for name, cp in copies.items():
            pl.when(has[name.rstrip("2")])(cp.start)

    def wait_send(copies):
        for name, cp in copies.items():
            pl.when(has[name.rstrip("2")])(cp.wait_send)

    def wait_recv(copies):
        for name, cp in copies.items():
            pl.when(has[opposite[name.rstrip("2")]])(cp.wait_recv)

    start(first)

    all31 = mrecv.at[0 : NGZ - 1, 0:2]
    pltpu.make_async_copy(all31, all31, ms).wait()
    pltpu.make_async_copy(all31, all31, mr).wait()

    lane = lax.broadcasted_iota(jnp.int32, (NGZ, LANE), 1)
    dev = lax.broadcasted_iota(jnp.int32, (NGZ, LANE), 0)
    got = mrecv[:, 1, :]
    gtab[...] = got
    mine = (lane == gz) | (lane == gz + 32)
    got = jnp.where(mine, got, -1)
    place = 2 * dev + jnp.where(lane == gz + 32, 1, 0)
    lane1 = lax.broadcasted_iota(jnp.int32, (8, LANE), 1)
    acc = jnp.zeros((8, LANE), jnp.int32)
    for s in range(32):
        total = jnp.sum(jnp.where(got == s, place, 0))
        acc = jnp.where(lane1 == s, total, acc)
    srcv[...] = jnp.minimum(acc, POS - 1)
    c1 = pltpu.make_async_copy(gtab, gs, lsem.at[0, 0])
    c2 = pltpu.make_async_copy(srcv, srcs, lsem.at[0, 1])
    c3 = pltpu.make_async_copy(bposv, bpos, lsem.at[1, 0])
    c1.start()
    c2.start()
    c3.start()

    row = lax.broadcasted_iota(jnp.int32, (CY, LANE), 0)
    lane16 = lax.broadcasted_iota(jnp.int32, (CY, LANE), 1)

    def ones(l, c):
        z = jnp.where(l < 3, l + 13, jnp.where(l < 19, l - 3, l - 19))
        who = jnp.where(l < 3, gz - 1, jnp.where(l < 19, gz, gz + 1))
        real = (who >= 0) & (who < NGZ)
        blk = mrecv[jnp.clip(who, 0, NGZ - 1), 0:1, :]
        blk = jnp.where(real, blk, -1)
        for xb in range(XB):
            hit = blk == z * 32 + row * 2 + xb
            start_row = pl.multiple_of(l * 32 + xb * 16, 16)
            onehot[pl.ds(start_row, 16), 0:128] = jnp.where(hit, 1.0, 0.0).astype(BF16)
            onehot[pl.ds(start_row, 16), 128:256] = jnp.where(hit & (lane16 < 64), 1.0, 0.0).astype(BF16)
        return c

    lax.fori_loop(0, CZ + 6, ones, 0)
    c1.wait()
    c2.wait()
    c3.wait()
    wait_send(first)
    wait_recv(first)

    def step(n, carry):
        p = lax.rem(n, 2)
        q = 1 - p

        def velocity(k, c):
            ks = k + S0
            for t in range(2):
                r0 = Y0 + 8 * t

                def s(f, xb, dz=0, dy=0):
                    return S[f, ks + dz, xb, pl.ds(r0 + dy, 8), :]

                xx = dx(s(0, 0), s(0, 1), True)
                xy = dx(s(2, 0), s(2, 1), False)
                xz = dx(s(5, 0), s(5, 1), False)
                for xb in range(XB):
                    fx = xx[xb] + dmaj(lambda o: s(2, xb, dy=o), False) + dmaj(lambda o: s(5, xb, dz=o), False)
                    fy = xy[xb] + dmaj(lambda o: s(1, xb, dy=o), True) + dmaj(lambda o: s(3, xb, dz=o), False)
                    fz = xz[xb] + dmaj(lambda o: s(3, xb, dy=o), False) + dmaj(lambda o: s(4, xb, dz=o), True)
                    bu = dtb[k, xb, pl.ds(8 * t, 8), :]
                    for f, force in enumerate((fx, fy, fz)):
                        new = V[p, f, k + V0, xb, pl.ds(r0, 8), :] + bu * force
                        own[f, k, xb, pl.ds(8 * t, 8), :] = new
            return c

        lax.fori_loop(0, CZ, velocity, 0, unroll=4)

        def pick(d, c):
            for u in range(2):
                b = bpos[0, u * 32 + d]
                z, y, xb = b // 32, (b // 2) % 16, b % 2
                for f in range(3):
                    bsend[2 * d + u, pl.ds(f, 1), :] = own[f, z, xb, pl.ds(y, 1), :]
            return c

        lax.fori_loop(0, NGZ, pick, 0, unroll=8)

        def b_copy(t):
            return remote(
                bsend.at[pl.ds(2 * t, 2), 0:3], brecv.at[pl.ds(2 * gz, 2), 0:3], bs, br, (t, gy)
            )

        for t in partners:
            b_copy(t).start()
        for u in range(2):
            brecv[2 * gz + u] = bsend[2 * gz + u]

        zc = {
            "down": remote(own.at[:, 0:3], V.at[q, :, 20:23, :, 14:30], zs.at[0], zr.at[q, 0], (down, gy)),
            "up": remote(own.at[:, 13:16], V.at[q, :, 1:4, :, 14:30], zs.at[1], zr.at[q, 1], (up, gy)),
        }
        start(zc)

        ball = brecv.at[0 : POS - 2, 0:3]
        pltpu.make_async_copy(ball, ball, br).wait()

        for j in range(16):
            side0 = brecv[srcs[0, 2 * j]]
            side1 = brecv[srcs[0, 2 * j + 1]]
            slip = side0 - side1
            traction = gain[0, 0, j] * slip / jnp.sqrt(1.0 + slip * slip)
            htab[2 * j] = -0.5 * traction
            htab[2 * j + 1] = 0.5 * traction

        def reply(d, c):
            for u in range(2):
                slot = gs[d, u * 32 + gz]
                slot = jnp.where((slot < 0) | (slot > 32), 32, slot)
                for f in range(3):
                    csend[f, pl.ds(2 * d + 2 + u, 1), :] = htab[slot, pl.ds(f, 1), :]
            return c

        lax.fori_loop(0, NGZ, reply, 0, unroll=8)

        def c_copy(t):
            return remote(csend.at[:, pl.ds(2 * t, 6)], crecv.at[:, pl.ds(6 * gz, 6)], cs, cr, (t, gy))

        for t in partners:
            c_copy(t).start()
        for u in range(6):
            for f in range(3):
                crecv[f, pl.ds(6 * gz + u, 1), :] = csend[f, pl.ds(2 * gz + u, 1), :]

        pltpu.make_async_copy(ball, ball, bs).wait()
        wait_send(zc)
        wait_recv(zc)
        call = crecv.at[:, 0 : 6 * (NGZ - 1)]
        pltpu.make_async_copy(call, call, cr).wait()

        for g in range(3):
            for f in range(3):
                col = pl.ds(f * LANE, LANE)
                d = jnp.concatenate(
                    [crecv[f, pl.ds(2 * g + r, NGZ, stride=6), :] for r in range(2)], axis=0
                )
                hi = d.astype(BF16)
                d = d - hi.astype(F32)
                mid = d.astype(BF16)
                lo = (d - mid.astype(F32)).astype(BF16)
                rhs[g, 0:64, col] = hi
                rhs[g, 64:128, col] = mid
                rhs[g, 128:192, col] = lo

        def apply(first_layer, layers, g):
            delta = jnp.dot(
                onehot[pl.ds(first_layer * 32, layers * 32), :], rhs[g], preferred_element_type=F32
            )
            for l in range(layers):
                at = first_layer + 1 + l
                for xb in range(XB):
                    for f in range(3):
                        r = l * 32 + xb * 16
                        here = own[f, at - V0, xb] if g == 1 else V[q, f, at, xb, pl.ds(Y0, CY), :]
                        V[q, f, at, xb, pl.ds(Y0, CY), :] = (
                            here + delta[r : r + 16, f * LANE : (f + 1) * LANE]
                        )

        apply(0, 3, 0)
        apply(19, 3, 2)
        apply(3, 8, 1)
        apply(11, 8, 1)
        pltpu.make_async_copy(call, call, cs).wait()

        yc = {
            "left": remote(V.at[q, :, 1:23, :, 14:17], V.at[q, :, 1:23, :, 30:33], ys.at[0], yr.at[q, 0], (gz, left)),
            "right": remote(V.at[q, :, 1:23, :, 27:30], V.at[q, :, 1:23, :, 11:14], ys.at[1], yr.at[q, 1], (gz, right)),
        }
        start(yc)

        def sensitivity(k, c):
            for f in range(3):
                for xb in range(XB):
                    sens[f, k, xb] = sens[f, k, xb] + DT * V[q, f, k + V0, xb, pl.ds(Y0, CY), :]
            return c

        lax.fori_loop(0, CZ, sensitivity, 0, unroll=4)

        def stress(tiles, k, c):
            kv = k + 2
            for t in tiles:
                r0 = 8 + 8 * t

                def v(f, xb, dz=0, dy=0):
                    return V[q, f, kv + dz, xb, pl.ds(r0 + dy, 8), :]

                exs = dx(v(0, 0), v(0, 1), False)
                vyx = dx(v(1, 0), v(1, 1), True)
                vzx = dx(v(2, 0), v(2, 1), True)
                for xb in range(XB):
                    ex = exs[xb]
                    ey = dmaj(lambda o: v(1, xb, dy=o), False)
                    ez = dmaj(lambda o: v(2, xb, dz=o), False)
                    la = S[6, k, xb, pl.ds(r0, 8), :]
                    mu = S[7, k, xb, pl.ds(r0, 8), :]
                    mu2 = mu + mu
                    div = la * (ex + ey + ez)
                    new = (
                        div + mu2 * ex,
                        div + mu2 * ey,
                        mu * (dmaj(lambda o: v(0, xb, dy=o), True) + vyx[xb]),
                        mu * (dmaj(lambda o: v(1, xb, dz=o), True) + dmaj(lambda o: v(2, xb, dy=o), True)),
                        div + mu2 * ez,
                        mu * (dmaj(lambda o: v(0, xb, dz=o), True) + vzx[xb]),
                    )
                    for f in range(6):
                        S[f, k, xb, pl.ds(r0, 8), :] = S[f, k, xb, pl.ds(r0, 8), :] + new[f]
            return c

        lax.fori_loop(0, SZ, functools.partial(stress, (1,)), 0, unroll=5)
        wait_send(yc)
        wait_recv(yc)
        lax.fori_loop(0, SZ, functools.partial(stress, (0, 2)), 0, unroll=4)
        return carry

    lax.fori_loop(0, STEPS, step, 0)

    last = STEPS % 2
    stores = []
    for xb in range(XB):
        cols = pl.ds(xb * LANE, LANE)
        stores.append(
            pltpu.make_async_copy(
                V.at[last, :, V0 : V0 + CZ, xb, Y0 : Y0 + CY, :], out.at[0:3, :, :, cols], lsem.at[0, xb]
            )
        )
        stores.append(
            pltpu.make_async_copy(
                S.at[0:6, S0 : S0 + CZ, xb, Y0 : Y0 + CY, :], out.at[3:9, :, :, cols], lsem.at[1, xb]
            )
        )
        stores.append(pltpu.make_async_copy(sens.at[:, :, xb], sens_out.at[:, :, :, cols], lsem.at[2, xb]))
    for cp in stores:
        cp.start()
    for cp in stores:
        cp.wait()


def per_device(state, region, lame, shear, buoyt, face_block, face_owner, face_slot, joint_gain):
    smem = pl.BlockSpec(memory_space=pltpu.SMEM)
    anym = pl.BlockSpec(memory_space=pl.ANY)
    hbm = pl.BlockSpec(memory_space=pltpu.HBM)
    dma = pltpu.SemaphoreType.DMA
    return pl.pallas_call(
        kernel,
        out_shape=(
            jax.ShapeDtypeStruct(state.shape, F32),
            jax.ShapeDtypeStruct((3,) + state.shape[1:], F32),
        ),
        in_specs=[hbm, hbm] + [smem] * 7,
        out_specs=(anym, anym),
        scratch_shapes=[
            pltpu.VMEM((2, 3, VZ, XB, YR, LANE), F32),
            pltpu.VMEM((8, SZ, XB, YR, LANE), F32),
            pltpu.VMEM((3, CZ, XB, CY, LANE), F32),
            pltpu.VMEM((CZ, XB, CY, LANE), F32),
            pltpu.VMEM((3, CZ, XB, CY, LANE), F32),
            pltpu.VMEM((CZ, XB, CY, LANE), jnp.int32),
            pltpu.VMEM((POS, 8, LANE), F32),
            pltpu.VMEM((POS, 8, LANE), F32),
            pltpu.VMEM((3, POS + 8, LANE), F32),
            pltpu.VMEM((3, 6 * NGZ, LANE), F32),
            pltpu.VMEM((33, 8, LANE), F32),
            pltpu.VMEM(((CZ + 6) * 32, 256), BF16),
            pltpu.VMEM((3, 256, 3 * LANE), BF16),
            pltpu.VMEM((8, LANE), jnp.int32),
            pltpu.VMEM((NGZ, 8, LANE), jnp.int32),
            pltpu.VMEM((NGZ, LANE), jnp.int32),
            pltpu.SMEM((NGZ, LANE), jnp.int32),
            pltpu.VMEM((8, LANE), jnp.int32),
            pltpu.SMEM((8, LANE), jnp.int32),
            pltpu.VMEM((8, LANE), jnp.int32),
            pltpu.SMEM((8, LANE), jnp.int32),
            dma((3, 2)),
            dma,
            dma,
            dma,
            dma,
            dma((2,)),
            dma((2, 2)),
            dma((2,)),
            dma((2, 2)),
            dma,
            dma,
            dma((6,)),
            dma((6,)),
        ],
        compiler_params=pltpu.CompilerParams(
            collective_id=0, has_side_effects=True, vmem_limit_bytes=60 * 1024 * 1024
        ),
    )(state, region, lame, shear, buoyt, face_block, face_owner, face_slot, joint_gain)


def solution(mesh):
    grid = P("gz", "gy", None)
    field = P(None, "gz", "gy", None)
    return jax.shard_map(
        per_device,
        mesh=mesh,
        in_specs=(field, grid, P(), P(), P(), grid, grid, grid, grid),
        out_specs=(field, field),
        check_vma=False,
    )
```

```python
import functools

import jax
import jax.numpy as jnp
from jax import lax
from jax.sharding import PartitionSpec as P
from jax.experimental import pallas as pl
from jax.experimental.pallas import tpu as pltpu

MESH = pl.DeviceIdType.MESH
STEPS = 12
CAP = 2
C1 = 9.0 / 8.0
C2 = -1.0 / 24.0
DT = 0.15
NGZ, NGY = 32, 4
CZ, CY, XB, LANE = 16, 16, 2, 128
POS = NGZ * CAP
YR, Y0 = 40, 14
VZ, V0 = CZ + 8, 4
SZ, S0 = CZ + 4, 2
F32 = jnp.float32
BF16 = jnp.bfloat16

OFFSETS = sorted(
    [(a, b, c) for a in range(2) for b in range(4) for c in range(4) if a + b + c > 0],
    key=lambda o: -(2 * o[0] + min(o[1], 4 - o[1]) + min(o[2], 4 - o[2])),
)


def xshift(f0, f1, by):
    lane = lax.broadcasted_iota(jnp.int32, f0.shape, 1)
    a = pltpu.roll(f0, (-by) % LANE, 1)
    b = pltpu.roll(f1, (-by) % LANE, 1)
    if by > 0:
        keep = lane < LANE - by
        return jnp.where(keep, a, b), jnp.where(keep, b, 0.0)
    keep = lane >= -by
    return jnp.where(keep, a, 0.0), jnp.where(keep, b, a)


def stencil(p, c, n, f, forward):
    return C1 * (n - c) + C2 * (f - p)


def dx(f0, f1, forward):
    up = xshift(f0, f1, 1)
    dn = xshift(f0, f1, -1)
    if forward:
        far = xshift(f0, f1, 2)
        return tuple(C1 * (up[i] - (f0, f1)[i]) + C2 * (far[i] - dn[i]) for i in range(2))
    far = xshift(f0, f1, -2)
    return tuple(C1 * ((f0, f1)[i] - dn[i]) + C2 * (up[i] - far[i]) for i in range(2))


def dmaj(load, forward):
    if forward:
        return C1 * (load(1) - load(0)) + C2 * (load(2) - load(-1))
    return C1 * (load(0) - load(-1)) + C2 * (load(1) - load(-2))


def kernel(
    state, region, lame, shear, buoyt, fblock, fowner, fslot, gain,
    out, sens_out,
    V, S, own, dtb, sens, reg, bsend, brecv, bloc, csend, crecv, htab, onehot, rhs,
    meta, mrecv, gtab, gs, srcv, srcs, bposv, bpos, gvec, gland, gtwin,
    lsem, bs, br, cs, cr, zs, zr, ys, yr, ms, mr, gsend, grecv, hs, hr,
):
    gz = lax.axis_index("gz")
    gy = lax.axis_index("gy")
    a0, b0, c0 = gz // 16, (gz // 4) % 4, gz % 4
    partners = [
        ((a0 + a) % 2) * 16 + ((b0 + b) % 4) * 4 + (c0 + c) % 4 for a, b, c in OFFSETS
    ]
    hh = gz % 16
    near = [
        (((b0 + b) % 4) * 4 + (c0 + c) % 4, b + c == 0) for b, c in sorted(
            [(b, c) for b in range(4) for c in range(4)],
            key=lambda o: -(min(o[0], 4 - o[0]) + min(o[1], 4 - o[1])),
        )
    ]
    down, up = (gz + NGZ - 1) % NGZ, (gz + 1) % NGZ
    left, right = (gy + NGY - 1) % NGY, (gy + 1) % NGY
    has = {"down": gz > 0, "up": gz < NGZ - 1, "left": gy > 0, "right": gy < NGY - 1}

    loads = []
    for xb in range(XB):
        cols = pl.ds(xb * LANE, LANE)
        loads.append(pltpu.make_async_copy(region.at[:, :, cols], reg.at[:, xb], lsem.at[0, xb]))
        loads.append(
            pltpu.make_async_copy(
                state.at[0:3, :, :, cols], V.at[0, :, V0 : V0 + CZ, xb, Y0 : Y0 + CY, :], lsem.at[1, xb]
            )
        )
        loads.append(
            pltpu.make_async_copy(
                state.at[3:9, :, :, cols], S.at[0:6, S0 : S0 + CZ, xb, Y0 : Y0 + CY, :], lsem.at[2, xb]
            )
        )
    for cp in loads:
        cp.start()

    zero = jnp.zeros((8, LANE), F32)
    zero16 = jnp.zeros((CY, LANE), F32)

    def edges(ref, idx):
        for xb in range(XB):
            ref[(*idx, xb, pl.ds(Y0 - 8, 8), slice(None))] = zero
            ref[(*idx, xb, pl.ds(Y0 + CY, 8), slice(None))] = zero

    def clear_v(l, c):
        for par in range(2):
            for f in range(3):
                edges(V, (par, f, l))
        return c

    lax.fori_loop(0, VZ, clear_v, 0)

    def clear_s(l, c):
        for f in range(8):
            edges(S, (f, l))
        return c

    lax.fori_loop(0, SZ, clear_s, 0)

    def clear_layers(l, c):
        for xb in range(XB):
            for base in (0, V0 + CZ):
                for par in range(2):
                    for f in range(3):
                        V[par, f, base + l, xb, pl.ds(Y0, CY), :] = zero16
        return c

    lax.fori_loop(0, V0, clear_layers, 0)
    for l in (0, 1, S0 + CZ, S0 + CZ + 1):
        for xb in range(XB):
            for f in range(8):
                S[f, l, xb, pl.ds(Y0, CY), :] = zero16
    for f in range(3):
        rhs[f, 192:256, :] = jnp.zeros((64, 384), BF16)
    htab[64] = zero
    gains = jnp.zeros((8, LANE), F32)
    for j in range(16):
        gains = jnp.where(lax.broadcasted_iota(jnp.int32, (8, LANE), 1) == j, gain[0, 0, j], gains)
    gvec[...] = gains

    lane8 = lax.broadcasted_iota(jnp.int32, (8, LANE), 1)
    lane_owner, lane_rank = lane8 % 32, (lane8 // 32) % 2
    count = jnp.zeros((8, LANE), jnp.int32)
    block_at = jnp.full((8, LANE), -1, jnp.int32)
    slot_at = jnp.full((8, LANE), -1, jnp.int32)
    for e in range(32):
        to = lane_owner == fowner[0, 0, e]
        here = to & (lane_rank == count)
        block_at = jnp.where(here, fblock[0, 0, e], block_at)
        slot_at = jnp.where(here, fslot[0, 0, e], slot_at)
        count = jnp.where(to, count + 1, count)
    sub = lax.broadcasted_iota(jnp.int32, (8, LANE), 0)
    meta[...] = jnp.where(sub == 0, block_at, slot_at)
    bposv[...] = jnp.clip(block_at, 0, 511)

    barrier = pltpu.get_barrier_semaphore()
    for t in partners:
        pl.semaphore_signal(barrier, inc=1, device_id=(t, gy), device_id_type=MESH)
    for t in range(1, NGY):
        pl.semaphore_signal(barrier, inc=1, device_id=(gz, (gy + t) % NGY), device_id_type=MESH)

    for cp in loads:
        cp.wait()

    def material(l, c):
        for xb in range(XB):
            r = reg[l, xb]
            la = jnp.zeros((CY, LANE), F32)
            mu = jnp.zeros((CY, LANE), F32)
            bu = jnp.zeros((CY, LANE), F32)
            for v in range(8):
                hit = r == v
                la = jnp.where(hit, DT * lame[v], la)
                mu = jnp.where(hit, DT * shear[v], mu)
                bu = jnp.where(hit, DT * buoyt[v], bu)
            S[6, S0 + l, xb, pl.ds(Y0, CY), :] = la
            S[7, S0 + l, xb, pl.ds(Y0, CY), :] = mu
            dtb[l, xb] = bu
            for f in range(3):
                sens[f, l, xb] = jnp.zeros((CY, LANE), F32)
        return c

    lax.fori_loop(0, CZ, material, 0)
    pl.semaphore_wait(barrier, NGZ - 1 + NGY - 1)

    def remote(src, dst, s, r, to):
        return pltpu.make_async_remote_copy(
            src, dst, send_sem=s, recv_sem=r, device_id=to, device_id_type=MESH
        )

    def meta_copy(t):
        return remote(meta.at[0:2], mrecv.at[gz, 0:2], ms, mr, (t, gy))

    for t in partners:
        meta_copy(t).start()
    mrecv[gz] = meta[...]
    gcopy = remote(gvec, gland, gsend, grecv, ((gz + 16) % NGZ, gy))
    gcopy.start()

    first = {
        "down": remote(S.at[3:8, 2:4, :, 14:30], S.at[3:8, 18:20, :, 14:30], hs.at[0], hr.at[0], (down, gy)),
        "up": remote(S.at[3:8, 16:18, :, 14:30], S.at[3:8, 0:2, :, 14:30], hs.at[1], hr.at[1], (up, gy)),
        "left": remote(S.at[1:4, 2:18, :, 14:16], S.at[1:4, 2:18, :, 30:32], hs.at[2], hr.at[2], (gz, left)),
        "right": remote(S.at[1:4, 2:18, :, 28:30], S.at[1:4, 2:18, :, 12:14], hs.at[3], hr.at[3], (gz, right)),
        "left2": remote(S.at[6:8, 2:18, :, 14:16], S.at[6:8, 2:18, :, 30:32], hs.at[4], hr.at[4], (gz, left)),
        "right2": remote(S.at[6:8, 2:18, :, 28:30], S.at[6:8, 2:18, :, 12:14], hs.at[5], hr.at[5], (gz, right)),
    }
    opposite = {"down": "up", "up": "down", "left": "right", "right": "left"}

    def start(copies):
        for name, cp in copies.items():
            pl.when(has[name.rstrip("2")])(cp.start)

    def wait_send(copies):
        for name, cp in copies.items():
            pl.when(has[name.rstrip("2")])(cp.wait_send)

    def wait_recv(copies):
        for name, cp in copies.items():
            pl.when(has[opposite[name.rstrip("2")]])(cp.wait_recv)

    start(first)

    all31 = mrecv.at[0 : NGZ - 1, 0:2]
    pltpu.make_async_copy(all31, all31, ms).wait()
    pltpu.make_async_copy(all31, all31, mr).wait()

    lane = lax.broadcasted_iota(jnp.int32, (NGZ, LANE), 1)
    dev = lax.broadcasted_iota(jnp.int32, (NGZ, LANE), 0)
    got = mrecv[:, 1, :]
    gtab[...] = got
    lane1 = lax.broadcasted_iota(jnp.int32, (8, LANE), 1)
    acc = jnp.zeros((8, LANE), jnp.int32)
    for e in range(2):
        role = hh + 16 * e
        of_role = jnp.where((lane == role) | (lane == role + 32), got, -1)
        place = 4 * dev + 2 * e + jnp.where(lane == role + 32, 1, 0)
        for s in range(32):
            total = jnp.sum(jnp.where(of_role == s, place, 0))
            acc = jnp.where((lane1 == s) & (sub == e), total, acc)
    srcv[...] = jnp.clip(acc, 0, 4 * NGZ - 1)
    gcopy.wait()
    c1 = pltpu.make_async_copy(gtab, gs, lsem.at[0, 0])
    c2 = pltpu.make_async_copy(srcv, srcs, lsem.at[0, 1])
    c3 = pltpu.make_async_copy(bposv, bpos, lsem.at[1, 0])
    c1.start()
    c2.start()
    c3.start()
    c4 = pltpu.make_async_copy(gland, gtwin, lsem.at[1, 1])
    c4.start()

    row = lax.broadcasted_iota(jnp.int32, (CY, LANE), 0)
    lane16 = lax.broadcasted_iota(jnp.int32, (CY, LANE), 1)

    def ones(l, c):
        z = jnp.where(l < 3, l + 13, jnp.where(l < 19, l - 3, l - 19))
        who = jnp.where(l < 3, gz - 1, jnp.where(l < 19, gz, gz + 1))
        real = (who >= 0) & (who < NGZ)
        blk = mrecv[jnp.clip(who, 0, NGZ - 1), 0:1, :]
        blk = jnp.where(real, blk, -1)
        for xb in range(XB):
            hit = blk == z * 32 + row * 2 + xb
            start_row = pl.multiple_of(l * 32 + xb * 16, 16)
            onehot[pl.ds(start_row, 16), 0:128] = jnp.where(hit, 1.0, 0.0).astype(BF16)
            onehot[pl.ds(start_row, 16), 128:256] = jnp.where(hit & (lane16 < 64), 1.0, 0.0).astype(BF16)
        return c

    lax.fori_loop(0, CZ + 6, ones, 0)
    c1.wait()
    c2.wait()
    c3.wait()
    c4.wait()
    wait_send(first)
    wait_recv(first)

    def step(n, carry):
        p = lax.rem(n, 2)
        q = 1 - p

        def velocity(k, c):
            ks = k + S0
            for t in range(2):
                r0 = Y0 + 8 * t

                def s(f, xb, dz=0, dy=0):
                    return S[f, ks + dz, xb, pl.ds(r0 + dy, 8), :]

                xx = dx(s(0, 0), s(0, 1), True)
                xy = dx(s(2, 0), s(2, 1), False)
                xz = dx(s(5, 0), s(5, 1), False)
                for xb in range(XB):
                    fx = xx[xb] + dmaj(lambda o: s(2, xb, dy=o), False) + dmaj(lambda o: s(5, xb, dz=o), False)
                    fy = xy[xb] + dmaj(lambda o: s(1, xb, dy=o), True) + dmaj(lambda o: s(3, xb, dz=o), False)
                    fz = xz[xb] + dmaj(lambda o: s(3, xb, dy=o), False) + dmaj(lambda o: s(4, xb, dz=o), True)
                    bu = dtb[k, xb, pl.ds(8 * t, 8), :]
                    for f, force in enumerate((fx, fy, fz)):
                        new = V[p, f, k + V0, xb, pl.ds(r0, 8), :] + bu * force
                        own[f, k, xb, pl.ds(8 * t, 8), :] = new
            return c

        lax.fori_loop(0, CZ, velocity, 0, unroll=4)

        for t, here in near:
            for e in range(2):
                for u in range(2):
                    b = bpos[0, u * 32 + e * 16 + t]
                    z, y, xb = b // 32, (b // 2) % 16, b % 2
                    for f in range(3):
                        bsend[4 * t + 2 * e + u, pl.ds(f, 1), :] = own[f, z, xb, pl.ds(y, 1), :]
            part = bsend.at[pl.ds(4 * t, 4), 0:3]
            place = brecv.at[q, pl.ds(4 * gz, 4), 0:3]
            remote(part, place, bs, br.at[q], (16 * (1 - a0) + t, gy)).start()
            if here:
                for u in range(4):
                    brecv[q, 4 * gz + u] = bsend[4 * t + u]
            else:
                remote(part, place, bs, br.at[q], (16 * a0 + t, gy)).start()

        zc = {
            "down": remote(own.at[:, 0:3], V.at[q, :, 20:23, :, 14:30], zs.at[0], zr.at[q, 0], (down, gy)),
            "up": remote(own.at[:, 13:16], V.at[q, :, 1:4, :, 14:30], zs.at[1], zr.at[q, 1], (up, gy)),
        }
        start(zc)

        ball = brecv.at[q, 0 : 4 * (NGZ - 1), 0:3]
        pltpu.make_async_copy(ball, ball, br.at[q]).wait()
        for d in range(4 * NGZ):
            bloc[d] = brecv[q, d]

        for e in range(2):
            for j in range(16):
                side0 = bloc[srcs[e, 2 * j]]
                side1 = bloc[srcs[e, 2 * j + 1]]
                slip = side0 - side1
                g = jnp.where(a0 == e, gain[0, 0, j], gtwin[0, j])
                traction = g * slip / jnp.sqrt(1.0 + slip * slip)
                htab[32 * e + 2 * j] = -0.5 * traction
                htab[32 * e + 2 * j + 1] = 0.5 * traction

        def reply(i, c):
            d = jnp.clip(16 * a0 - 1 + i, 0, NGZ - 1)
            for e in range(2):
                for u in range(2):
                    slot = gs[d, u * 32 + hh + 16 * e]
                    slot = jnp.where((slot < 0) | (slot > 31), 64, slot + 32 * e)
                    for f in range(3):
                        csend[f, e, pl.ds(2 * i + u, 1), :] = htab[slot, pl.ds(f, 1), :]
            return c

        lax.fori_loop(0, 18, reply, 0, unroll=6)

        for t, here in near:
            if here:
                for u in range(6):
                    for f in range(3):
                        for e in range(2):
                            crecv[f, e, pl.ds(6 * hh + u, 1), :] = csend[f, e, pl.ds(2 * hh + u, 1), :]
            else:
                remote(
                    csend.at[:, :, pl.ds(2 * t, 6)], crecv.at[:, :, pl.ds(6 * hh, 6)], cs, cr, (16 * a0 + t, gy)
                ).start()

        pltpu.make_async_copy(ball, ball, bs).wait()
        wait_send(zc)
        wait_recv(zc)
        call = crecv.at[:, :, 0:90]
        pltpu.make_async_copy(call, call, cr).wait()

        for g in range(3):
            for f in range(3):
                col = pl.ds(f * LANE, LANE)
                d = jnp.concatenate(
                    [crecv[f, e, pl.ds(2 * g + r, 16, stride=6), :] for r in range(2) for e in range(2)], axis=0
                )
                hi = d.astype(BF16)
                d = d - hi.astype(F32)
                mid = d.astype(BF16)
                lo = (d - mid.astype(F32)).astype(BF16)
                rhs[g, 0:64, col] = hi
                rhs[g, 64:128, col] = mid
                rhs[g, 128:192, col] = lo

        def apply(first_layer, layers, g):
            delta = jnp.dot(
                onehot[pl.ds(first_layer * 32, layers * 32), :], rhs[g], preferred_element_type=F32
            )
            for l in range(layers):
                at = first_layer + 1 + l
                for xb in range(XB):
                    for f in range(3):
                        r = l * 32 + xb * 16
                        here = own[f, at - V0, xb] if g == 1 else V[q, f, at, xb, pl.ds(Y0, CY), :]
                        V[q, f, at, xb, pl.ds(Y0, CY), :] = (
                            here + delta[r : r + 16, f * LANE : (f + 1) * LANE]
                        )

        apply(0, 3, 0)
        apply(19, 3, 2)
        apply(3, 8, 1)
        apply(11, 8, 1)
        pltpu.make_async_copy(call, call, cs).wait()

        yc = {
            "left2": remote(V.at[q, 1:3, 2:22, :, 14:17], V.at[q, 1:3, 2:22, :, 30:33], ys.at[2], yr.at[q, 2], (gz, left)),
            "right2": remote(V.at[q, 1:3, 2:22, :, 27:30], V.at[q, 1:3, 2:22, :, 11:14], ys.at[3], yr.at[q, 3], (gz, right)),
            "left": remote(V.at[q, 0, 4:20, :, 14:17], V.at[q, 0, 4:20, :, 30:33], ys.at[0], yr.at[q, 0], (gz, left)),
            "right": remote(V.at[q, 0, 4:20, :, 27:30], V.at[q, 0, 4:20, :, 11:14], ys.at[1], yr.at[q, 1], (gz, right)),
        }
        start(yc)

        def sensitivity(k, c):
            for f in range(3):
                for xb in range(XB):
                    sens[f, k, xb] = sens[f, k, xb] + DT * V[q, f, k + V0, xb, pl.ds(Y0, CY), :]
            return c

        lax.fori_loop(0, CZ, sensitivity, 0, unroll=4)

        def stress(tiles, k, c):
            kv = k + 2
            for t in tiles:
                r0 = 8 + 8 * t

                def v(f, xb, dz=0, dy=0):
                    return V[q, f, kv + dz, xb, pl.ds(r0 + dy, 8), :]

                exs = dx(v(0, 0), v(0, 1), False)
                vyx = dx(v(1, 0), v(1, 1), True)
                vzx = dx(v(2, 0), v(2, 1), True)
                for xb in range(XB):
                    ex = exs[xb]
                    ey = dmaj(lambda o: v(1, xb, dy=o), False)
                    ez = dmaj(lambda o: v(2, xb, dz=o), False)
                    la = S[6, k, xb, pl.ds(r0, 8), :]
                    mu = S[7, k, xb, pl.ds(r0, 8), :]
                    mu2 = mu + mu
                    div = la * (ex + ey + ez)
                    new = (
                        div + mu2 * ex,
                        div + mu2 * ey,
                        mu * (dmaj(lambda o: v(0, xb, dy=o), True) + vyx[xb]),
                        mu * (dmaj(lambda o: v(1, xb, dz=o), True) + dmaj(lambda o: v(2, xb, dy=o), True)),
                        div + mu2 * ez,
                        mu * (dmaj(lambda o: v(0, xb, dz=o), True) + vzx[xb]),
                    )
                    for f in range(6):
                        S[f, k, xb, pl.ds(r0, 8), :] = S[f, k, xb, pl.ds(r0, 8), :] + new[f]
            return c

        lax.fori_loop(0, SZ, functools.partial(stress, (1,)), 0, unroll=5)
        wait_send(yc)
        wait_recv(yc)
        lax.fori_loop(0, SZ, functools.partial(stress, (0, 2)), 0, unroll=4)
        return carry

    lax.fori_loop(0, STEPS, step, 0)

    last = STEPS % 2
    stores = []
    for xb in range(XB):
        cols = pl.ds(xb * LANE, LANE)
        stores.append(
            pltpu.make_async_copy(
                V.at[last, :, V0 : V0 + CZ, xb, Y0 : Y0 + CY, :], out.at[0:3, :, :, cols], lsem.at[0, xb]
            )
        )
        stores.append(
            pltpu.make_async_copy(
                S.at[0:6, S0 : S0 + CZ, xb, Y0 : Y0 + CY, :], out.at[3:9, :, :, cols], lsem.at[1, xb]
            )
        )
        stores.append(pltpu.make_async_copy(sens.at[:, :, xb], sens_out.at[:, :, :, cols], lsem.at[2, xb]))
    for cp in stores:
        cp.start()
    for cp in stores:
        cp.wait()


def per_device(state, region, lame, shear, buoyt, face_block, face_owner, face_slot, joint_gain):
    smem = pl.BlockSpec(memory_space=pltpu.SMEM)
    anym = pl.BlockSpec(memory_space=pl.ANY)
    hbm = pl.BlockSpec(memory_space=pltpu.HBM)
    dma = pltpu.SemaphoreType.DMA
    return pl.pallas_call(
        kernel,
        out_shape=(
            jax.ShapeDtypeStruct(state.shape, F32),
            jax.ShapeDtypeStruct((3,) + state.shape[1:], F32),
        ),
        in_specs=[hbm, hbm] + [smem] * 7,
        out_specs=(anym, anym),
        scratch_shapes=[
            pltpu.VMEM((2, 3, VZ, XB, YR, LANE), F32),
            pltpu.VMEM((8, SZ, XB, YR, LANE), F32),
            pltpu.VMEM((3, CZ, XB, CY, LANE), F32),
            pltpu.VMEM((CZ, XB, CY, LANE), F32),
            pltpu.VMEM((3, CZ, XB, CY, LANE), F32),
            pltpu.VMEM((CZ, XB, CY, LANE), jnp.int32),
            pltpu.VMEM((POS, 8, LANE), F32),
            pltpu.VMEM((2, 4 * NGZ, 8, LANE), F32),
            pltpu.VMEM((4 * NGZ, 8, LANE), F32),
            pltpu.VMEM((3, 2, 40, LANE), F32),
            pltpu.VMEM((3, 2, 96, LANE), F32),
            pltpu.VMEM((65, 8, LANE), F32),
            pltpu.VMEM(((CZ + 6) * 32, 256), BF16),
            pltpu.VMEM((3, 256, 3 * LANE), BF16),
            pltpu.VMEM((8, LANE), jnp.int32),
            pltpu.VMEM((NGZ, 8, LANE), jnp.int32),
            pltpu.VMEM((NGZ, LANE), jnp.int32),
            pltpu.SMEM((NGZ, LANE), jnp.int32),
            pltpu.VMEM((8, LANE), jnp.int32),
            pltpu.SMEM((8, LANE), jnp.int32),
            pltpu.VMEM((8, LANE), jnp.int32),
            pltpu.SMEM((8, LANE), jnp.int32),
            pltpu.VMEM((8, LANE), F32),
            pltpu.VMEM((8, LANE), F32),
            pltpu.SMEM((8, LANE), F32),
            dma((3, 2)),
            dma,
            dma((2,)),
            dma,
            dma,
            dma((2,)),
            dma((2, 2)),
            dma((4,)),
            dma((2, 4)),
            dma,
            dma,
            dma,
            dma,
            dma((6,)),
            dma((6,)),
        ],
        compiler_params=pltpu.CompilerParams(
            collective_id=0, has_side_effects=True, vmem_limit_bytes=60 * 1024 * 1024
        ),
    )(state, region, lame, shear, buoyt, face_block, face_owner, face_slot, joint_gain)


def solution(mesh):
    grid = P("gz", "gy", None)
    field = P(None, "gz", "gy", None)
    return jax.shard_map(
        per_device,
        mesh=mesh,
        in_specs=(field, grid, P(), P(), P(), grid, grid, grid, grid),
        out_specs=(field, field),
        check_vma=False,
    )
```

```python
import functools

import jax
import jax.numpy as jnp
from jax import lax
from jax.sharding import PartitionSpec as P
from jax.experimental import pallas as pl
from jax.experimental.pallas import tpu as pltpu

MESH = pl.DeviceIdType.MESH
STEPS = 12
CAP = 2
C1 = 9.0 / 8.0
C2 = -1.0 / 24.0
DT = 0.15
NGZ, NGY = 32, 4
CZ, CY, XB, LANE = 16, 16, 2, 128
POS = NGZ * CAP
YR, Y0 = 40, 14
VZ, V0 = CZ + 8, 4
SZ, S0 = CZ + 4, 2
F32 = jnp.float32
BF16 = jnp.bfloat16

OFFSETS = sorted(
    [(a, b, c) for a in range(2) for b in range(4) for c in range(4) if a + b + c > 0],
    key=lambda o: -(2 * o[0] + min(o[1], 4 - o[1]) + min(o[2], 4 - o[2])),
)


def xshift(f0, f1, by):
    lane = lax.broadcasted_iota(jnp.int32, f0.shape, 1)
    a = pltpu.roll(f0, (-by) % LANE, 1)
    b = pltpu.roll(f1, (-by) % LANE, 1)
    if by > 0:
        keep = lane < LANE - by
        return jnp.where(keep, a, b), jnp.where(keep, b, 0.0)
    keep = lane >= -by
    return jnp.where(keep, a, 0.0), jnp.where(keep, b, a)


def stencil(p, c, n, f, forward):
    return C1 * (n - c) + C2 * (f - p)


def dx(f0, f1, forward):
    up = xshift(f0, f1, 1)
    dn = xshift(f0, f1, -1)
    if forward:
        far = xshift(f0, f1, 2)
        return tuple(C1 * (up[i] - (f0, f1)[i]) + C2 * (far[i] - dn[i]) for i in range(2))
    far = xshift(f0, f1, -2)
    return tuple(C1 * ((f0, f1)[i] - dn[i]) + C2 * (up[i] - far[i]) for i in range(2))


def dmaj(load, forward):
    if forward:
        return C1 * (load(1) - load(0)) + C2 * (load(2) - load(-1))
    return C1 * (load(0) - load(-1)) + C2 * (load(1) - load(-2))


def kernel(
    state, region, lame, shear, buoyt, fblock, fowner, fslot, gain,
    out, sens_out,
    V, S, own, dtb, sens, reg, bsend, brecv, bloc, csend, crecv, htab, onehot, rhs,
    meta, mrecv, gtab, gs, srcv, srcs, bposv, bpos, gvec, gland, gtwin,
    lsem, bs, br, cs, cr, zs, zr, ys, yr, ms, mr, gsend, grecv, hs, hr,
):
    gz = lax.axis_index("gz")
    gy = lax.axis_index("gy")
    a0, b0, c0 = gz // 16, (gz // 4) % 4, gz % 4
    partners = [
        ((a0 + a) % 2) * 16 + ((b0 + b) % 4) * 4 + (c0 + c) % 4 for a, b, c in OFFSETS
    ]
    hh = gz % 16
    near = [
        (((b0 + b) % 4) * 4 + (c0 + c) % 4, b + c == 0) for b, c in sorted(
            [(b, c) for b in range(4) for c in range(4)],
            key=lambda o: -(min(o[0], 4 - o[0]) + min(o[1], 4 - o[1])),
        )
    ]
    down, up = (gz + NGZ - 1) % NGZ, (gz + 1) % NGZ
    left, right = (gy + NGY - 1) % NGY, (gy + 1) % NGY
    has = {"down": gz > 0, "up": gz < NGZ - 1, "left": gy > 0, "right": gy < NGY - 1}

    loads = []
    for xb in range(XB):
        cols = pl.ds(xb * LANE, LANE)
        loads.append(pltpu.make_async_copy(region.at[:, :, cols], reg.at[:, xb], lsem.at[0, xb]))
        loads.append(
            pltpu.make_async_copy(
                state.at[0:3, :, :, cols], V.at[0, :, V0 : V0 + CZ, xb, Y0 : Y0 + CY, :], lsem.at[1, xb]
            )
        )
        loads.append(
            pltpu.make_async_copy(
                state.at[3:9, :, :, cols], S.at[0:6, S0 : S0 + CZ, xb, Y0 : Y0 + CY, :], lsem.at[2, xb]
            )
        )
    for cp in loads:
        cp.start()

    zero = jnp.zeros((8, LANE), F32)
    zero16 = jnp.zeros((CY, LANE), F32)

    def edges(ref, idx):
        for xb in range(XB):
            ref[(*idx, xb, pl.ds(Y0 - 8, 8), slice(None))] = zero
            ref[(*idx, xb, pl.ds(Y0 + CY, 8), slice(None))] = zero

    def clear_v(l, c):
        for par in range(2):
            for f in range(3):
                edges(V, (par, f, l))
        return c

    lax.fori_loop(0, VZ, clear_v, 0)

    def clear_s(l, c):
        for f in range(8):
            edges(S, (f, l))
        return c

    lax.fori_loop(0, SZ, clear_s, 0)

    def clear_layers(l, c):
        for xb in range(XB):
            for base in (0, V0 + CZ):
                for par in range(2):
                    for f in range(3):
                        V[par, f, base + l, xb, pl.ds(Y0, CY), :] = zero16
        return c

    lax.fori_loop(0, V0, clear_layers, 0)
    for l in (0, 1, S0 + CZ, S0 + CZ + 1):
        for xb in range(XB):
            for f in range(8):
                S[f, l, xb, pl.ds(Y0, CY), :] = zero16
    for f in range(3):
        rhs[f, 192:256, :] = jnp.zeros((64, 384), BF16)
    htab[64] = zero
    gains = jnp.zeros((8, LANE), F32)
    for j in range(16):
        gains = jnp.where(lax.broadcasted_iota(jnp.int32, (8, LANE), 1) == j, gain[0, 0, j], gains)
    gvec[...] = gains

    lane8 = lax.broadcasted_iota(jnp.int32, (8, LANE), 1)
    lane_owner, lane_rank = lane8 % 32, (lane8 // 32) % 2
    count = jnp.zeros((8, LANE), jnp.int32)
    block_at = jnp.full((8, LANE), -1, jnp.int32)
    slot_at = jnp.full((8, LANE), -1, jnp.int32)
    for e in range(32):
        to = lane_owner == fowner[0, 0, e]
        here = to & (lane_rank == count)
        block_at = jnp.where(here, fblock[0, 0, e], block_at)
        slot_at = jnp.where(here, fslot[0, 0, e], slot_at)
        count = jnp.where(to, count + 1, count)
    sub = lax.broadcasted_iota(jnp.int32, (8, LANE), 0)
    meta[...] = jnp.where(sub == 0, block_at, slot_at)
    bposv[...] = jnp.clip(block_at, 0, 511)

    barrier = pltpu.get_barrier_semaphore()
    for t in partners:
        pl.semaphore_signal(barrier, inc=1, device_id=(t, gy), device_id_type=MESH)
    for t in range(1, NGY):
        pl.semaphore_signal(barrier, inc=1, device_id=(gz, (gy + t) % NGY), device_id_type=MESH)

    for cp in loads:
        cp.wait()

    def material(l, c):
        for xb in range(XB):
            r = reg[l, xb]
            la = jnp.zeros((CY, LANE), F32)
            mu = jnp.zeros((CY, LANE), F32)
            bu = jnp.zeros((CY, LANE), F32)
            for v in range(8):
                hit = r == v
                la = jnp.where(hit, DT * lame[v], la)
                mu = jnp.where(hit, DT * shear[v], mu)
                bu = jnp.where(hit, DT * buoyt[v], bu)
            S[6, S0 + l, xb, pl.ds(Y0, CY), :] = la
            S[7, S0 + l, xb, pl.ds(Y0, CY), :] = mu
            dtb[l, xb] = bu
            for f in range(3):
                sens[f, l, xb] = jnp.zeros((CY, LANE), F32)
        return c

    lax.fori_loop(0, CZ, material, 0)
    pl.semaphore_wait(barrier, NGZ - 1 + NGY - 1)

    def remote(src, dst, s, r, to):
        return pltpu.make_async_remote_copy(
            src, dst, send_sem=s, recv_sem=r, device_id=to, device_id_type=MESH
        )

    def meta_copy(t):
        return remote(meta.at[0:2], mrecv.at[gz, 0:2], ms, mr, (t, gy))

    for t in partners:
        meta_copy(t).start()
    mrecv[gz] = meta[...]
    gcopy = remote(gvec, gland, gsend, grecv, ((gz + 16) % NGZ, gy))
    gcopy.start()

    first = {
        "down": remote(S.at[3:8, 2:4, :, 14:30], S.at[3:8, 18:20, :, 14:30], hs.at[0], hr.at[0], (down, gy)),
        "up": remote(S.at[3:8, 16:18, :, 14:30], S.at[3:8, 0:2, :, 14:30], hs.at[1], hr.at[1], (up, gy)),
        "left": remote(S.at[1:4, 2:18, :, 14:16], S.at[1:4, 2:18, :, 30:32], hs.at[2], hr.at[2], (gz, left)),
        "right": remote(S.at[1:4, 2:18, :, 28:30], S.at[1:4, 2:18, :, 12:14], hs.at[3], hr.at[3], (gz, right)),
        "left2": remote(S.at[6:8, 2:18, :, 14:16], S.at[6:8, 2:18, :, 30:32], hs.at[4], hr.at[4], (gz, left)),
        "right2": remote(S.at[6:8, 2:18, :, 28:30], S.at[6:8, 2:18, :, 12:14], hs.at[5], hr.at[5], (gz, right)),
    }
    opposite = {"down": "up", "up": "down", "left": "right", "right": "left"}

    def start(copies):
        for name, cp in copies.items():
            pl.when(has[name.rstrip("2")])(cp.start)

    def wait_send(copies):
        for name, cp in copies.items():
            pl.when(has[name.rstrip("2")])(cp.wait_send)

    def wait_recv(copies):
        for name, cp in copies.items():
            pl.when(has[opposite[name.rstrip("2")]])(cp.wait_recv)

    start(first)

    all31 = mrecv.at[0 : NGZ - 1, 0:2]
    pltpu.make_async_copy(all31, all31, ms).wait()
    pltpu.make_async_copy(all31, all31, mr).wait()

    lane = lax.broadcasted_iota(jnp.int32, (NGZ, LANE), 1)
    dev = lax.broadcasted_iota(jnp.int32, (NGZ, LANE), 0)
    got = mrecv[:, 1, :]
    gtab[...] = got
    lane1 = lax.broadcasted_iota(jnp.int32, (8, LANE), 1)
    acc = jnp.zeros((8, LANE), jnp.int32)
    for e in range(2):
        role = hh + 16 * e
        of_role = jnp.where((lane == role) | (lane == role + 32), got, -1)
        place = 4 * dev + 2 * e + jnp.where(lane == role + 32, 1, 0)
        for s in range(32):
            total = jnp.sum(jnp.where(of_role == s, place, 0))
            acc = jnp.where((lane1 == s) & (sub == e), total, acc)
    srcv[...] = jnp.clip(acc, 0, 4 * NGZ - 1)
    gcopy.wait()
    c1 = pltpu.make_async_copy(gtab, gs, lsem.at[0, 0])
    c2 = pltpu.make_async_copy(srcv, srcs, lsem.at[0, 1])
    c3 = pltpu.make_async_copy(bposv, bpos, lsem.at[1, 0])
    c1.start()
    c2.start()
    c3.start()
    c4 = pltpu.make_async_copy(gland, gtwin, lsem.at[1, 1])
    c4.start()

    row = lax.broadcasted_iota(jnp.int32, (CY, LANE), 0)
    lane16 = lax.broadcasted_iota(jnp.int32, (CY, LANE), 1)

    def ones(l, c):
        z = jnp.where(l < 3, l + 13, jnp.where(l < 19, l - 3, l - 19))
        who = jnp.where(l < 3, gz - 1, jnp.where(l < 19, gz, gz + 1))
        real = (who >= 0) & (who < NGZ)
        blk = mrecv[jnp.clip(who, 0, NGZ - 1), 0:1, :]
        blk = jnp.where(real, blk, -1)
        for xb in range(XB):
            hit = blk == z * 32 + row * 2 + xb
            start_row = pl.multiple_of(l * 32 + xb * 16, 16)
            onehot[pl.ds(start_row, 16), 0:128] = jnp.where(hit, 1.0, 0.0).astype(BF16)
            onehot[pl.ds(start_row, 16), 128:256] = jnp.where(hit & (lane16 < 64), 1.0, 0.0).astype(BF16)
        return c

    lax.fori_loop(0, CZ + 6, ones, 0)
    c1.wait()
    c2.wait()
    c3.wait()
    c4.wait()
    wait_send(first)
    wait_recv(first)

    def step(n, carry):
        p = lax.rem(n, 2)
        q = 1 - p

        def velocity(k, c):
            ks = k + S0
            for t in range(2):
                r0 = Y0 + 8 * t

                def s(f, xb, dz=0, dy=0):
                    return S[f, ks + dz, xb, pl.ds(r0 + dy, 8), :]

                xx = dx(s(0, 0), s(0, 1), True)
                xy = dx(s(2, 0), s(2, 1), False)
                xz = dx(s(5, 0), s(5, 1), False)
                for xb in range(XB):
                    fx = xx[xb] + dmaj(lambda o: s(2, xb, dy=o), False) + dmaj(lambda o: s(5, xb, dz=o), False)
                    fy = xy[xb] + dmaj(lambda o: s(1, xb, dy=o), True) + dmaj(lambda o: s(3, xb, dz=o), False)
                    fz = xz[xb] + dmaj(lambda o: s(3, xb, dy=o), False) + dmaj(lambda o: s(4, xb, dz=o), True)
                    bu = dtb[k, xb, pl.ds(8 * t, 8), :]
                    for f, force in enumerate((fx, fy, fz)):
                        new = V[p, f, k + V0, xb, pl.ds(r0, 8), :] + bu * force
                        own[f, k, xb, pl.ds(8 * t, 8), :] = new
            return c

        lax.fori_loop(0, CZ, velocity, 0, unroll=4)

        for t, here in near:
            for e in range(2):
                for u in range(2):
                    b = bpos[0, u * 32 + e * 16 + t]
                    z, y, xb = b // 32, (b // 2) % 16, b % 2
                    for f in range(3):
                        bsend[4 * t + 2 * e + u, pl.ds(f, 1), :] = own[f, z, xb, pl.ds(y, 1), :]
            part = bsend.at[pl.ds(4 * t, 4), 0:3]
            place = brecv.at[q, pl.ds(4 * gz, 4), 0:3]
            remote(part, place, bs, br.at[q], (16 * (1 - a0) + t, gy)).start()
            if here:
                for u in range(4):
                    brecv[q, 4 * gz + u] = bsend[4 * t + u]
            else:
                remote(part, place, bs, br.at[q], (16 * a0 + t, gy)).start()

        zc = {
            "down": remote(own.at[:, 0:3], V.at[q, :, 20:23, :, 14:30], zs.at[0], zr.at[q, 0], (down, gy)),
            "up": remote(own.at[:, 13:16], V.at[q, :, 1:4, :, 14:30], zs.at[1], zr.at[q, 1], (up, gy)),
        }
        start(zc)

        ball = brecv.at[q, 0 : 4 * (NGZ - 1), 0:3]
        pltpu.make_async_copy(ball, ball, br.at[q]).wait()
        for d in range(4 * NGZ):
            bloc[d] = brecv[q, d]

        for e in range(2):
            for j in range(16):
                side0 = bloc[srcs[e, 2 * j]]
                side1 = bloc[srcs[e, 2 * j + 1]]
                slip = side0 - side1
                g = jnp.where(a0 == e, gain[0, 0, j], gtwin[0, j])
                traction = g * slip / jnp.sqrt(1.0 + slip * slip)
                htab[32 * e + 2 * j] = -0.5 * traction
                htab[32 * e + 2 * j + 1] = 0.5 * traction

        def reply(i, c):
            d = jnp.clip(16 * a0 - 1 + i, 0, NGZ - 1)
            for e in range(2):
                for u in range(2):
                    slot = gs[d, u * 32 + hh + 16 * e]
                    slot = jnp.where((slot < 0) | (slot > 31), 64, slot + 32 * e)
                    for f in range(3):
                        csend[f, e, pl.ds(2 * i + u, 1), :] = htab[slot, pl.ds(f, 1), :]
            return c

        lax.fori_loop(0, 18, reply, 0, unroll=6)

        for t, here in near:
            if here:
                for u in range(6):
                    for f in range(3):
                        for e in range(2):
                            crecv[f, e, pl.ds(6 * hh + u, 1), :] = csend[f, e, pl.ds(2 * hh + u, 1), :]
            else:
                remote(
                    csend.at[:, :, pl.ds(2 * t, 6)], crecv.at[:, :, pl.ds(6 * hh, 6)], cs, cr, (16 * a0 + t, gy)
                ).start()

        pltpu.make_async_copy(ball, ball, bs).wait()
        wait_send(zc)
        wait_recv(zc)
        call = crecv.at[:, :, 0:90]
        pltpu.make_async_copy(call, call, cr).wait()

        def terms(g):
            for f in range(3):
                col = pl.ds(f * LANE, LANE)
                d = jnp.concatenate(
                    [crecv[f, e, pl.ds(2 * g + r, 16, stride=6), :] for r in range(2) for e in range(2)], axis=0
                )
                hi = d.astype(BF16)
                d = d - hi.astype(F32)
                mid = d.astype(BF16)
                lo = (d - mid.astype(F32)).astype(BF16)
                rhs[g, 0:64, col] = hi
                rhs[g, 64:128, col] = mid
                rhs[g, 128:192, col] = lo

        def apply(first_layer, layers, g):
            delta = jnp.dot(
                onehot[pl.ds(first_layer * 32, layers * 32), :], rhs[g], preferred_element_type=F32
            )
            for l in range(layers):
                at = first_layer + 1 + l
                for xb in range(XB):
                    for f in range(3):
                        r = l * 32 + xb * 16
                        here = own[f, at - V0, xb] if g == 1 else V[q, f, at, xb, pl.ds(Y0, CY), :]
                        V[q, f, at, xb, pl.ds(Y0, CY), :] = (
                            here + delta[r : r + 16, f * LANE : (f + 1) * LANE]
                        )

        def strips(part, fields, layers):
            low, high = V.at[q, fields, layers, :, 14:17], V.at[q, fields, layers, :, 27:30]
            after, before = V.at[q, fields, layers, :, 30:33], V.at[q, fields, layers, :, 11:14]
            return {
                "left": remote(low, after, ys.at[0, part], yr.at[q, 0, part], (gz, left)),
                "right": remote(high, before, ys.at[1, part], yr.at[q, 1, part], (gz, right)),
            }

        yc = [
            strips(0, slice(0, 3), slice(4, 12)),
            strips(1, slice(0, 3), slice(12, 20)),
            strips(2, slice(1, 3), slice(2, 4)),
            strips(3, slice(1, 3), slice(20, 22)),
        ]
        terms(1)
        apply(3, 8, 1)
        start(yc[0])
        apply(11, 8, 1)
        start(yc[1])
        terms(0)
        apply(0, 3, 0)
        start(yc[2])
        terms(2)
        apply(19, 3, 2)
        start(yc[3])
        pltpu.make_async_copy(call, call, cs).wait()

        def sensitivity(k, c):
            for f in range(3):
                for xb in range(XB):
                    sens[f, k, xb] = sens[f, k, xb] + DT * V[q, f, k + V0, xb, pl.ds(Y0, CY), :]
            return c

        lax.fori_loop(0, CZ, sensitivity, 0, unroll=4)

        def stress(tiles, k, c):
            kv = k + 2
            for t in tiles:
                r0 = 8 + 8 * t

                def v(f, xb, dz=0, dy=0):
                    return V[q, f, kv + dz, xb, pl.ds(r0 + dy, 8), :]

                exs = dx(v(0, 0), v(0, 1), False)
                vyx = dx(v(1, 0), v(1, 1), True)
                vzx = dx(v(2, 0), v(2, 1), True)
                for xb in range(XB):
                    ex = exs[xb]
                    ey = dmaj(lambda o: v(1, xb, dy=o), False)
                    ez = dmaj(lambda o: v(2, xb, dz=o), False)
                    la = S[6, k, xb, pl.ds(r0, 8), :]
                    mu = S[7, k, xb, pl.ds(r0, 8), :]
                    mu2 = mu + mu
                    div = la * (ex + ey + ez)
                    new = (
                        div + mu2 * ex,
                        div + mu2 * ey,
                        mu * (dmaj(lambda o: v(0, xb, dy=o), True) + vyx[xb]),
                        mu * (dmaj(lambda o: v(1, xb, dz=o), True) + dmaj(lambda o: v(2, xb, dy=o), True)),
                        div + mu2 * ez,
                        mu * (dmaj(lambda o: v(0, xb, dz=o), True) + vzx[xb]),
                    )
                    for f in range(6):
                        S[f, k, xb, pl.ds(r0, 8), :] = S[f, k, xb, pl.ds(r0, 8), :] + new[f]
            return c

        lax.fori_loop(0, SZ, functools.partial(stress, (1,)), 0, unroll=5)
        for part in yc:
            wait_send(part)
            wait_recv(part)
        lax.fori_loop(0, SZ, functools.partial(stress, (0, 2)), 0, unroll=4)
        return carry

    lax.fori_loop(0, STEPS, step, 0)

    last = STEPS % 2
    stores = []
    for xb in range(XB):
        cols = pl.ds(xb * LANE, LANE)
        stores.append(
            pltpu.make_async_copy(
                V.at[last, :, V0 : V0 + CZ, xb, Y0 : Y0 + CY, :], out.at[0:3, :, :, cols], lsem.at[0, xb]
            )
        )
        stores.append(
            pltpu.make_async_copy(
                S.at[0:6, S0 : S0 + CZ, xb, Y0 : Y0 + CY, :], out.at[3:9, :, :, cols], lsem.at[1, xb]
            )
        )
        stores.append(pltpu.make_async_copy(sens.at[:, :, xb], sens_out.at[:, :, :, cols], lsem.at[2, xb]))
    for cp in stores:
        cp.start()
    for cp in stores:
        cp.wait()


def per_device(state, region, lame, shear, buoyt, face_block, face_owner, face_slot, joint_gain):
    smem = pl.BlockSpec(memory_space=pltpu.SMEM)
    anym = pl.BlockSpec(memory_space=pl.ANY)
    hbm = pl.BlockSpec(memory_space=pltpu.HBM)
    dma = pltpu.SemaphoreType.DMA
    return pl.pallas_call(
        kernel,
        out_shape=(
            jax.ShapeDtypeStruct(state.shape, F32),
            jax.ShapeDtypeStruct((3,) + state.shape[1:], F32),
        ),
        in_specs=[hbm, hbm] + [smem] * 7,
        out_specs=(anym, anym),
        scratch_shapes=[
            pltpu.VMEM((2, 3, VZ, XB, YR, LANE), F32),
            pltpu.VMEM((8, SZ, XB, YR, LANE), F32),
            pltpu.VMEM((3, CZ, XB, CY, LANE), F32),
            pltpu.VMEM((CZ, XB, CY, LANE), F32),
            pltpu.VMEM((3, CZ, XB, CY, LANE), F32),
            pltpu.VMEM((CZ, XB, CY, LANE), jnp.int32),
            pltpu.VMEM((POS, 8, LANE), F32),
            pltpu.VMEM((2, 4 * NGZ, 8, LANE), F32),
            pltpu.VMEM((4 * NGZ, 8, LANE), F32),
            pltpu.VMEM((3, 2, 40, LANE), F32),
            pltpu.VMEM((3, 2, 96, LANE), F32),
            pltpu.VMEM((65, 8, LANE), F32),
            pltpu.VMEM(((CZ + 6) * 32, 256), BF16),
            pltpu.VMEM((3, 256, 3 * LANE), BF16),
            pltpu.VMEM((8, LANE), jnp.int32),
            pltpu.VMEM((NGZ, 8, LANE), jnp.int32),
            pltpu.VMEM((NGZ, LANE), jnp.int32),
            pltpu.SMEM((NGZ, LANE), jnp.int32),
            pltpu.VMEM((8, LANE), jnp.int32),
            pltpu.SMEM((8, LANE), jnp.int32),
            pltpu.VMEM((8, LANE), jnp.int32),
            pltpu.SMEM((8, LANE), jnp.int32),
            pltpu.VMEM((8, LANE), F32),
            pltpu.VMEM((8, LANE), F32),
            pltpu.SMEM((8, LANE), F32),
            dma((3, 2)),
            dma,
            dma((2,)),
            dma,
            dma,
            dma((2,)),
            dma((2, 2)),
            dma((2, 4)),
            dma((2, 2, 4)),
            dma,
            dma,
            dma,
            dma,
            dma((6,)),
            dma((6,)),
        ],
        compiler_params=pltpu.CompilerParams(
            collective_id=0, has_side_effects=True, vmem_limit_bytes=60 * 1024 * 1024
        ),
    )(state, region, lame, shear, buoyt, face_block, face_owner, face_slot, joint_gain)


def solution(mesh):
    grid = P("gz", "gy", None)
    field = P(None, "gz", "gy", None)
    return jax.shard_map(
        per_device,
        mesh=mesh,
        in_specs=(field, grid, P(), P(), P(), grid, grid, grid, grid),
        out_specs=(field, field),
        check_vma=False,
    )
```

```python
import functools

import jax
import jax.numpy as jnp
from jax import lax
from jax.sharding import PartitionSpec as P
from jax.experimental import pallas as pl
from jax.experimental.pallas import tpu as pltpu

MESH = pl.DeviceIdType.MESH
STEPS = 12
CAP = 2
C1 = 9.0 / 8.0
C2 = -1.0 / 24.0
DT = 0.15
NGZ, NGY = 32, 4
CZ, CY, XB, LANE = 16, 16, 2, 128
POS = NGZ * CAP
YR, Y0 = 40, 14
VZ, V0 = CZ + 8, 4
SZ, S0 = CZ + 4, 2
F32 = jnp.float32
BF16 = jnp.bfloat16

OFFSETS = sorted(
    [(a, b, c) for a in range(2) for b in range(4) for c in range(4) if a + b + c > 0],
    key=lambda o: -(2 * o[0] + min(o[1], 4 - o[1]) + min(o[2], 4 - o[2])),
)


def xshift(f0, f1, by):
    lane = lax.broadcasted_iota(jnp.int32, f0.shape, 1)
    a = pltpu.roll(f0, (-by) % LANE, 1)
    b = pltpu.roll(f1, (-by) % LANE, 1)
    if by > 0:
        keep = lane < LANE - by
        return jnp.where(keep, a, b), jnp.where(keep, b, 0.0)
    keep = lane >= -by
    return jnp.where(keep, a, 0.0), jnp.where(keep, b, a)


def stencil(p, c, n, f, forward):
    return C1 * (n - c) + C2 * (f - p)


def dx(f0, f1, forward):
    up = xshift(f0, f1, 1)
    dn = xshift(f0, f1, -1)
    if forward:
        far = xshift(f0, f1, 2)
        return tuple(C1 * (up[i] - (f0, f1)[i]) + C2 * (far[i] - dn[i]) for i in range(2))
    far = xshift(f0, f1, -2)
    return tuple(C1 * ((f0, f1)[i] - dn[i]) + C2 * (up[i] - far[i]) for i in range(2))


def dmaj(load, forward):
    if forward:
        return C1 * (load(1) - load(0)) + C2 * (load(2) - load(-1))
    return C1 * (load(0) - load(-1)) + C2 * (load(1) - load(-2))


def kernel(
    state, region, lame, shear, buoyt, fblock, fowner, fslot, gain,
    out, sens_out,
    V, S, own, dtb, sens, reg, bsend, brecv, bloc, csend, crecv, htab, onehot, rhs,
    meta, mrecv, gtab, gs, srcv, srcs, bposv, bpos, gvec, gland, gtwin,
    lsem, bs, br, cs, cr, zs, zr, ys, yr, ms, mr, gsend, grecv, hs, hr,
):
    gz = lax.axis_index("gz")
    gy = lax.axis_index("gy")
    a0, b0, c0 = gz // 16, (gz // 4) % 4, gz % 4
    partners = [
        ((a0 + a) % 2) * 16 + ((b0 + b) % 4) * 4 + (c0 + c) % 4 for a, b, c in OFFSETS
    ]
    hh = gz % 16
    near = [
        (((b0 + b) % 4) * 4 + (c0 + c) % 4, b + c == 0) for b, c in sorted(
            [(b, c) for b in range(4) for c in range(4)],
            key=lambda o: -(min(o[0], 4 - o[0]) + min(o[1], 4 - o[1])),
        )
    ]
    down, up = (gz + NGZ - 1) % NGZ, (gz + 1) % NGZ
    left, right = (gy + NGY - 1) % NGY, (gy + 1) % NGY
    has = {"down": gz > 0, "up": gz < NGZ - 1, "left": gy > 0, "right": gy < NGY - 1}

    loads = []
    for xb in range(XB):
        cols = pl.ds(xb * LANE, LANE)
        loads.append(pltpu.make_async_copy(region.at[:, :, cols], reg.at[:, xb], lsem.at[0, xb]))
        loads.append(
            pltpu.make_async_copy(
                state.at[0:3, :, :, cols], V.at[0, :, V0 : V0 + CZ, xb, Y0 : Y0 + CY, :], lsem.at[1, xb]
            )
        )
        loads.append(
            pltpu.make_async_copy(
                state.at[3:9, :, :, cols], S.at[0:6, S0 : S0 + CZ, xb, Y0 : Y0 + CY, :], lsem.at[2, xb]
            )
        )
    for cp in loads:
        cp.start()

    zero = jnp.zeros((8, LANE), F32)
    zero16 = jnp.zeros((CY, LANE), F32)

    def edges(ref, idx):
        for xb in range(XB):
            ref[(*idx, xb, pl.ds(Y0 - 8, 8), slice(None))] = zero
            ref[(*idx, xb, pl.ds(Y0 + CY, 8), slice(None))] = zero

    def clear_v(l, c):
        for par in range(2):
            for f in range(3):
                edges(V, (par, f, l))
        return c

    lax.fori_loop(0, VZ, clear_v, 0)

    def clear_s(l, c):
        for f in range(8):
            edges(S, (f, l))
        return c

    lax.fori_loop(0, SZ, clear_s, 0)

    def clear_layers(l, c):
        for xb in range(XB):
            for base in (0, V0 + CZ):
                for par in range(2):
                    for f in range(3):
                        V[par, f, base + l, xb, pl.ds(Y0, CY), :] = zero16
        return c

    lax.fori_loop(0, V0, clear_layers, 0)
    for l in (0, 1, S0 + CZ, S0 + CZ + 1):
        for xb in range(XB):
            for f in range(8):
                S[f, l, xb, pl.ds(Y0, CY), :] = zero16
    for f in range(3):
        rhs[f, 192:256, :] = jnp.zeros((64, 384), BF16)
    htab[64] = zero
    gains = jnp.zeros((8, LANE), F32)
    for j in range(16):
        gains = jnp.where(lax.broadcasted_iota(jnp.int32, (8, LANE), 1) == j, gain[0, 0, j], gains)
    gvec[...] = gains

    lane8 = lax.broadcasted_iota(jnp.int32, (8, LANE), 1)
    lane_owner, lane_rank = lane8 % 32, (lane8 // 32) % 2
    count = jnp.zeros((8, LANE), jnp.int32)
    block_at = jnp.full((8, LANE), -1, jnp.int32)
    slot_at = jnp.full((8, LANE), -1, jnp.int32)
    for e in range(32):
        to = lane_owner == fowner[0, 0, e]
        here = to & (lane_rank == count)
        block_at = jnp.where(here, fblock[0, 0, e], block_at)
        slot_at = jnp.where(here, fslot[0, 0, e], slot_at)
        count = jnp.where(to, count + 1, count)
    sub = lax.broadcasted_iota(jnp.int32, (8, LANE), 0)
    meta[...] = jnp.where(sub == 0, block_at, slot_at)
    bposv[...] = jnp.clip(block_at, 0, 511)

    barrier = pltpu.get_barrier_semaphore()
    for t in partners:
        pl.semaphore_signal(barrier, inc=1, device_id=(t, gy), device_id_type=MESH)
    for t in range(1, NGY):
        pl.semaphore_signal(barrier, inc=1, device_id=(gz, (gy + t) % NGY), device_id_type=MESH)

    for cp in loads:
        cp.wait()

    def material(l, c):
        for xb in range(XB):
            r = reg[l, xb]
            la = jnp.zeros((CY, LANE), F32)
            mu = jnp.zeros((CY, LANE), F32)
            bu = jnp.zeros((CY, LANE), F32)
            for v in range(8):
                hit = r == v
                la = jnp.where(hit, DT * lame[v], la)
                mu = jnp.where(hit, DT * shear[v], mu)
                bu = jnp.where(hit, DT * buoyt[v], bu)
            S[6, S0 + l, xb, pl.ds(Y0, CY), :] = la
            S[7, S0 + l, xb, pl.ds(Y0, CY), :] = mu
            dtb[l, xb] = bu
            for f in range(3):
                sens[f, l, xb] = jnp.zeros((CY, LANE), F32)
        return c

    lax.fori_loop(0, CZ, material, 0)
    pl.semaphore_wait(barrier, NGZ - 1 + NGY - 1)

    def remote(src, dst, s, r, to):
        return pltpu.make_async_remote_copy(
            src, dst, send_sem=s, recv_sem=r, device_id=to, device_id_type=MESH
        )

    def meta_copy(t):
        return remote(meta.at[0:2], mrecv.at[gz, 0:2], ms, mr, (t, gy))

    for t in partners:
        meta_copy(t).start()
    mrecv[gz] = meta[...]
    gcopy = remote(gvec, gland, gsend, grecv, ((gz + 16) % NGZ, gy))
    gcopy.start()

    first = {
        "down": remote(S.at[3:8, 2:4, :, 14:30], S.at[3:8, 18:20, :, 14:30], hs.at[0], hr.at[0], (down, gy)),
        "up": remote(S.at[3:8, 16:18, :, 14:30], S.at[3:8, 0:2, :, 14:30], hs.at[1], hr.at[1], (up, gy)),
        "left": remote(S.at[1:4, 2:18, :, 14:16], S.at[1:4, 2:18, :, 30:32], hs.at[2], hr.at[2], (gz, left)),
        "right": remote(S.at[1:4, 2:18, :, 28:30], S.at[1:4, 2:18, :, 12:14], hs.at[3], hr.at[3], (gz, right)),
        "left2": remote(S.at[6:8, 2:18, :, 14:16], S.at[6:8, 2:18, :, 30:32], hs.at[4], hr.at[4], (gz, left)),
        "right2": remote(S.at[6:8, 2:18, :, 28:30], S.at[6:8, 2:18, :, 12:14], hs.at[5], hr.at[5], (gz, right)),
    }
    opposite = {"down": "up", "up": "down", "left": "right", "right": "left"}

    def start(copies):
        for name, cp in copies.items():
            pl.when(has[name.rstrip("2")])(cp.start)

    def wait_send(copies):
        for name, cp in copies.items():
            pl.when(has[name.rstrip("2")])(cp.wait_send)

    def wait_recv(copies):
        for name, cp in copies.items():
            pl.when(has[opposite[name.rstrip("2")]])(cp.wait_recv)

    start(first)

    all31 = mrecv.at[0 : NGZ - 1, 0:2]
    pltpu.make_async_copy(all31, all31, ms).wait()
    pltpu.make_async_copy(all31, all31, mr).wait()

    lane = lax.broadcasted_iota(jnp.int32, (NGZ, LANE), 1)
    dev = lax.broadcasted_iota(jnp.int32, (NGZ, LANE), 0)
    got = mrecv[:, 1, :]
    gtab[...] = got
    lane1 = lax.broadcasted_iota(jnp.int32, (8, LANE), 1)
    acc = jnp.zeros((8, LANE), jnp.int32)
    for e in range(2):
        role = hh + 16 * e
        of_role = jnp.where((lane == role) | (lane == role + 32), got, -1)
        place = 4 * dev + 2 * e + jnp.where(lane == role + 32, 1, 0)
        for s in range(32):
            total = jnp.sum(jnp.where(of_role == s, place, 0))
            acc = jnp.where((lane1 == s) & (sub == e), total, acc)
    srcv[...] = jnp.clip(acc, 0, 4 * NGZ - 1)
    gcopy.wait()
    c1 = pltpu.make_async_copy(gtab, gs, lsem.at[0, 0])
    c2 = pltpu.make_async_copy(srcv, srcs, lsem.at[0, 1])
    c3 = pltpu.make_async_copy(bposv, bpos, lsem.at[1, 0])
    c1.start()
    c2.start()
    c3.start()
    c4 = pltpu.make_async_copy(gland, gtwin, lsem.at[1, 1])
    c4.start()

    row = lax.broadcasted_iota(jnp.int32, (CY, LANE), 0)
    lane16 = lax.broadcasted_iota(jnp.int32, (CY, LANE), 1)

    def ones(l, c):
        z = jnp.where(l < 3, l + 13, jnp.where(l < 19, l - 3, l - 19))
        who = jnp.where(l < 3, gz - 1, jnp.where(l < 19, gz, gz + 1))
        real = (who >= 0) & (who < NGZ)
        blk = mrecv[jnp.clip(who, 0, NGZ - 1), 0:1, :]
        blk = jnp.where(real, blk, -1)
        for xb in range(XB):
            hit = blk == z * 32 + row * 2 + xb
            start_row = pl.multiple_of(l * 32 + xb * 16, 16)
            onehot[pl.ds(start_row, 16), 0:128] = jnp.where(hit, 1.0, 0.0).astype(BF16)
            onehot[pl.ds(start_row, 16), 128:256] = jnp.where(hit & (lane16 < 64), 1.0, 0.0).astype(BF16)
        return c

    lax.fori_loop(0, CZ + 6, ones, 0)
    c1.wait()
    c2.wait()
    c3.wait()
    c4.wait()
    wait_send(first)
    wait_recv(first)

    def step(n, carry):
        p = lax.rem(n, 2)
        q = 1 - p

        def velocity(k, c):
            ks = k + S0
            for t in range(2):
                r0 = Y0 + 8 * t

                def s(f, xb, dz=0, dy=0):
                    return S[f, ks + dz, xb, pl.ds(r0 + dy, 8), :]

                xx = dx(s(0, 0), s(0, 1), True)
                xy = dx(s(2, 0), s(2, 1), False)
                xz = dx(s(5, 0), s(5, 1), False)
                for xb in range(XB):
                    fx = xx[xb] + dmaj(lambda o: s(2, xb, dy=o), False) + dmaj(lambda o: s(5, xb, dz=o), False)
                    fy = xy[xb] + dmaj(lambda o: s(1, xb, dy=o), True) + dmaj(lambda o: s(3, xb, dz=o), False)
                    fz = xz[xb] + dmaj(lambda o: s(3, xb, dy=o), False) + dmaj(lambda o: s(4, xb, dz=o), True)
                    bu = dtb[k, xb, pl.ds(8 * t, 8), :]
                    for f, force in enumerate((fx, fy, fz)):
                        new = V[p, f, k + V0, xb, pl.ds(r0, 8), :] + bu * force
                        own[f, k, xb, pl.ds(8 * t, 8), :] = new
            return c

        lax.fori_loop(0, CZ, velocity, 0, unroll=4)

        for t, here in near:
            for e in range(2):
                for u in range(2):
                    b = bpos[0, u * 32 + e * 16 + t]
                    z, y, xb = b // 32, (b // 2) % 16, b % 2
                    for f in range(3):
                        bsend[4 * t + 2 * e + u, pl.ds(f, 1), :] = own[f, z, xb, pl.ds(y, 1), :]
            part = bsend.at[pl.ds(4 * t, 4), 0:3]
            place = brecv.at[q, pl.ds(4 * gz, 4), 0:3]
            remote(part, place, bs, br.at[q], (16 * (1 - a0) + t, gy)).start()
            if here:
                for u in range(4):
                    brecv[q, 4 * gz + u] = bsend[4 * t + u]
            else:
                remote(part, place, bs, br.at[q], (16 * a0 + t, gy)).start()

        zc = {
            "down": remote(own.at[:, 0:3], V.at[q, :, 20:23, :, 14:30], zs.at[0], zr.at[q, 0], (down, gy)),
            "up": remote(own.at[:, 13:16], V.at[q, :, 1:4, :, 14:30], zs.at[1], zr.at[q, 1], (up, gy)),
        }
        start(zc)

        ball = brecv.at[q, 0 : 4 * (NGZ - 1), 0:3]
        pltpu.make_async_copy(ball, ball, br.at[q]).wait()
        for d in range(4 * NGZ):
            bloc[d] = brecv[q, d]

        for e in range(2):
            for j in range(16):
                side0 = bloc[srcs[e, 2 * j]]
                side1 = bloc[srcs[e, 2 * j + 1]]
                slip = side0 - side1
                g = jnp.where(a0 == e, gain[0, 0, j], gtwin[0, j])
                traction = g * slip / jnp.sqrt(1.0 + slip * slip)
                htab[32 * e + 2 * j] = -0.5 * traction
                htab[32 * e + 2 * j + 1] = 0.5 * traction

        def reply(i, c):
            d = jnp.clip(16 * a0 - 1 + i, 0, NGZ - 1)
            for e in range(2):
                for u in range(2):
                    slot = gs[d, u * 32 + hh + 16 * e]
                    slot = jnp.where((slot < 0) | (slot > 31), 64, slot + 32 * e)
                    for f in range(3):
                        csend[f, e, pl.ds(2 * i + u, 1), :] = htab[slot, pl.ds(f, 1), :]
            return c

        lax.fori_loop(0, 18, reply, 0, unroll=6)

        for t, here in near:
            if here:
                for u in range(6):
                    for f in range(3):
                        for e in range(2):
                            crecv[f, e, pl.ds(6 * hh + u, 1), :] = csend[f, e, pl.ds(2 * hh + u, 1), :]
            else:
                remote(
                    csend.at[:, :, pl.ds(2 * t, 6)], crecv.at[:, :, pl.ds(6 * hh, 6)], cs, cr, (16 * a0 + t, gy)
                ).start()

        pltpu.make_async_copy(ball, ball, bs).wait()
        call = crecv.at[:, :, 0:90]
        pltpu.make_async_copy(call, call, cr).wait()

        def terms(g):
            for f in range(3):
                col = pl.ds(f * LANE, LANE)
                d = jnp.concatenate(
                    [crecv[f, e, pl.ds(2 * g + r, 16, stride=6), :] for r in range(2) for e in range(2)], axis=0
                )
                hi = d.astype(BF16)
                d = d - hi.astype(F32)
                mid = d.astype(BF16)
                lo = (d - mid.astype(F32)).astype(BF16)
                rhs[g, 0:64, col] = hi
                rhs[g, 64:128, col] = mid
                rhs[g, 128:192, col] = lo

        def apply(first_layer, layers, g):
            delta = jnp.dot(
                onehot[pl.ds(first_layer * 32, layers * 32), :], rhs[g], preferred_element_type=F32
            )
            for l in range(layers):
                at = first_layer + 1 + l
                for xb in range(XB):
                    for f in range(3):
                        r = l * 32 + xb * 16
                        here = own[f, at - V0, xb] if g == 1 else V[q, f, at, xb, pl.ds(Y0, CY), :]
                        V[q, f, at, xb, pl.ds(Y0, CY), :] = (
                            here + delta[r : r + 16, f * LANE : (f + 1) * LANE]
                        )

        def strips(part, fields, layers):
            low, high = V.at[q, fields, layers, :, 14:17], V.at[q, fields, layers, :, 27:30]
            after, before = V.at[q, fields, layers, :, 30:33], V.at[q, fields, layers, :, 11:14]
            return {
                "left": remote(low, after, ys.at[0, part], yr.at[q, 0, part], (gz, left)),
                "right": remote(high, before, ys.at[1, part], yr.at[q, 1, part], (gz, right)),
            }

        yc = [
            strips(0, slice(0, 3), slice(4, 12)),
            strips(1, slice(0, 3), slice(12, 20)),
            strips(2, slice(1, 3), slice(2, 4)),
            strips(3, slice(1, 3), slice(20, 22)),
        ]
        terms(1)
        apply(3, 8, 1)
        start(yc[0])
        apply(11, 8, 1)
        start(yc[1])
        wait_send(zc)
        wait_recv(zc)
        terms(0)
        apply(0, 3, 0)
        start(yc[2])
        terms(2)
        apply(19, 3, 2)
        start(yc[3])
        pltpu.make_async_copy(call, call, cs).wait()

        def sensitivity(k, c):
            for f in range(3):
                for xb in range(XB):
                    sens[f, k, xb] = sens[f, k, xb] + DT * V[q, f, k + V0, xb, pl.ds(Y0, CY), :]
            return c

        lax.fori_loop(0, CZ, sensitivity, 0, unroll=4)

        def stress(tiles, k, c):
            kv = k + 2
            for t in tiles:
                r0 = 8 + 8 * t

                def v(f, xb, dz=0, dy=0):
                    return V[q, f, kv + dz, xb, pl.ds(r0 + dy, 8), :]

                exs = dx(v(0, 0), v(0, 1), False)
                vyx = dx(v(1, 0), v(1, 1), True)
                vzx = dx(v(2, 0), v(2, 1), True)
                for xb in range(XB):
                    ex = exs[xb]
                    ey = dmaj(lambda o: v(1, xb, dy=o), False)
                    ez = dmaj(lambda o: v(2, xb, dz=o), False)
                    la = S[6, k, xb, pl.ds(r0, 8), :]
                    mu = S[7, k, xb, pl.ds(r0, 8), :]
                    mu2 = mu + mu
                    div = la * (ex + ey + ez)
                    new = (
                        div + mu2 * ex,
                        div + mu2 * ey,
                        mu * (dmaj(lambda o: v(0, xb, dy=o), True) + vyx[xb]),
                        mu * (dmaj(lambda o: v(1, xb, dz=o), True) + dmaj(lambda o: v(2, xb, dy=o), True)),
                        div + mu2 * ez,
                        mu * (dmaj(lambda o: v(0, xb, dz=o), True) + vzx[xb]),
                    )
                    for f in range(6):
                        S[f, k, xb, pl.ds(r0, 8), :] = S[f, k, xb, pl.ds(r0, 8), :] + new[f]
            return c

        lax.fori_loop(0, SZ, functools.partial(stress, (1,)), 0, unroll=5)
        for part in yc:
            wait_send(part)
            wait_recv(part)
        lax.fori_loop(0, SZ, functools.partial(stress, (0, 2)), 0, unroll=4)
        return carry

    lax.fori_loop(0, STEPS, step, 0)

    last = STEPS % 2
    stores = []
    for xb in range(XB):
        cols = pl.ds(xb * LANE, LANE)
        stores.append(
            pltpu.make_async_copy(
                V.at[last, :, V0 : V0 + CZ, xb, Y0 : Y0 + CY, :], out.at[0:3, :, :, cols], lsem.at[0, xb]
            )
        )
        stores.append(
            pltpu.make_async_copy(
                S.at[0:6, S0 : S0 + CZ, xb, Y0 : Y0 + CY, :], out.at[3:9, :, :, cols], lsem.at[1, xb]
            )
        )
        stores.append(pltpu.make_async_copy(sens.at[:, :, xb], sens_out.at[:, :, :, cols], lsem.at[2, xb]))
    for cp in stores:
        cp.start()
    for cp in stores:
        cp.wait()


def per_device(state, region, lame, shear, buoyt, face_block, face_owner, face_slot, joint_gain):
    smem = pl.BlockSpec(memory_space=pltpu.SMEM)
    anym = pl.BlockSpec(memory_space=pl.ANY)
    hbm = pl.BlockSpec(memory_space=pltpu.HBM)
    dma = pltpu.SemaphoreType.DMA
    return pl.pallas_call(
        kernel,
        out_shape=(
            jax.ShapeDtypeStruct(state.shape, F32),
            jax.ShapeDtypeStruct((3,) + state.shape[1:], F32),
        ),
        in_specs=[hbm, hbm] + [smem] * 7,
        out_specs=(anym, anym),
        scratch_shapes=[
            pltpu.VMEM((2, 3, VZ, XB, YR, LANE), F32),
            pltpu.VMEM((8, SZ, XB, YR, LANE), F32),
            pltpu.VMEM((3, CZ, XB, CY, LANE), F32),
            pltpu.VMEM((CZ, XB, CY, LANE), F32),
            pltpu.VMEM((3, CZ, XB, CY, LANE), F32),
            pltpu.VMEM((CZ, XB, CY, LANE), jnp.int32),
            pltpu.VMEM((POS, 8, LANE), F32),
            pltpu.VMEM((2, 4 * NGZ, 8, LANE), F32),
            pltpu.VMEM((4 * NGZ, 8, LANE), F32),
            pltpu.VMEM((3, 2, 40, LANE), F32),
            pltpu.VMEM((3, 2, 96, LANE), F32),
            pltpu.VMEM((65, 8, LANE), F32),
            pltpu.VMEM(((CZ + 6) * 32, 256), BF16),
            pltpu.VMEM((3, 256, 3 * LANE), BF16),
            pltpu.VMEM((8, LANE), jnp.int32),
            pltpu.VMEM((NGZ, 8, LANE), jnp.int32),
            pltpu.VMEM((NGZ, LANE), jnp.int32),
            pltpu.SMEM((NGZ, LANE), jnp.int32),
            pltpu.VMEM((8, LANE), jnp.int32),
            pltpu.SMEM((8, LANE), jnp.int32),
            pltpu.VMEM((8, LANE), jnp.int32),
            pltpu.SMEM((8, LANE), jnp.int32),
            pltpu.VMEM((8, LANE), F32),
            pltpu.VMEM((8, LANE), F32),
            pltpu.SMEM((8, LANE), F32),
            dma((3, 2)),
            dma,
            dma((2,)),
            dma,
            dma,
            dma((2,)),
            dma((2, 2)),
            dma((2, 4)),
            dma((2, 2, 4)),
            dma,
            dma,
            dma,
            dma,
            dma((6,)),
            dma((6,)),
        ],
        compiler_params=pltpu.CompilerParams(
            collective_id=0, has_side_effects=True, vmem_limit_bytes=60 * 1024 * 1024
        ),
    )(state, region, lame, shear, buoyt, face_block, face_owner, face_slot, joint_gain)


def solution(mesh):
    grid = P("gz", "gy", None)
    field = P(None, "gz", "gy", None)
    return jax.shard_map(
        per_device,
        mesh=mesh,
        in_specs=(field, grid, P(), P(), P(), grid, grid, grid, grid),
        out_specs=(field, field),
        check_vma=False,
    )
```
